512 devices in a mesh: context: 32 (over z, y_lo, core), tensor: 16 (over x, y_hi).
Axes of the slice: x: 4, y: 8 (y_hi: 4, y_lo: 2; y = y_hi * 2 + y_lo), z: 8, core: 2. Of those that a mesh axis runs over, the one named last changes fastest.
Arguments:
- x_in: bfloat16 [8192, 8192], P('context', 'tensor'), may hold values from -6 to 6
- grad_out: bfloat16 [8192, 8192], P('context', 'tensor'), may hold values from -6 to 6
- step_size: float32 [128, 8192], P('tensor', 'context'), may hold values from 0 to 1, as said below
- log_decay: float32 [128, 8192], P('tensor', 'context'), may hold values from -1 to 0, as said below
- b_proj: bfloat16 [2048, 8192], P('tensor', 'context'), may hold values from -0.375 to 0.375
- c_proj: bfloat16 [2048, 8192], P('tensor', 'context'), may hold values from -0.375 to 0.375
- w_in: bfloat16 [8192, 4096], P('tensor'), may hold values from -0.125 to 0.125
Outputs:
- grad_input: bfloat16 [4096, 8192], P('tensor', 'context')
- grad_b: bfloat16 [2048, 8192], P('tensor', 'context')
- grad_c: bfloat16 [2048, 8192], P('tensor', 'context')
The draws below stay inside these ranges and needn't reach their ends.
Inputs may be any that keep to these rules, and one draw needn't show every extreme that they name: `step_size`: every entry is positive. `log_decay`: every entry is below zero.
All inputs are finite; a program needn't handle non-finite values.
Results may differ from the reference program's by a relative error of at most 0.025.
Values may be sent and summed in bfloat16 or wider, within the bound.
No kernel may reach another device: no remote copies, remote signals or barrier semaphores. Data moves between devices by JAX's collectives and lax.ppermute only.
A program may use at most 128 MiB of HBM per device.

```python
import math
import jax
import jax.numpy as jnp
from jax import lax

D = 4096
HEAD_DIM = 64
STATE = 256
HEADS_DEV = 8
TOK_DEV = 256
HEADS = 128
GROUPS = 8
SEQUENCE_LENGTH = 8192
N_CONTEXT = 32
N_TENSOR = 16


def draw_step_size(key, part):
    key = jax.random.fold_in(key, 11)
    base = jnp.exp(jax.random.uniform(key, (HEADS, SEQUENCE_LENGTH), jnp.float32, math.log(0.5), math.log(2.0)))
    return base * (4.0 / math.sqrt(SEQUENCE_LENGTH))


def draw_log_decay(key, part):
    key = jax.random.fold_in(key, 23)
    key_rate, key_jitter, key_block, key_spots, key_loss = jax.random.split(key, 5)
    lowest = math.log(0.25 / SEQUENCE_LENGTH)
    highest = math.log(1.0 / 30.0)
    decay_rate = jnp.exp(jax.random.uniform(key_rate, (HEADS, 1), jnp.float32, lowest, highest))
    random_noise = jnp.exp(jax.random.uniform(key_jitter, (HEADS, SEQUENCE_LENGTH), jnp.float32, math.log(0.5), math.log(2.0)))
    block_multiplier = jnp.exp(jax.random.uniform(key_block, (HEADS, SEQUENCE_LENGTH // TOK_DEV, 1), jnp.float32, math.log(0.5), math.log(2.0)))
    block_multiplier = jnp.broadcast_to(block_multiplier, (HEADS, SEQUENCE_LENGTH // TOK_DEV, TOK_DEV)).reshape(HEADS, SEQUENCE_LENGTH)
    spike_positions = jax.random.randint(key_spots, (4,), 0, SEQUENCE_LENGTH)
    spike_amount = jnp.any(jnp.arange(SEQUENCE_LENGTH)[None, :] == spike_positions[:, None], axis=0)
    loss_value = jax.random.uniform(key_loss, (HEADS, SEQUENCE_LENGTH), jnp.float32, 0.22, 0.69)
    return -(decay_rate * random_noise * block_multiplier) - jnp.where(spike_amount[None, :], loss_value, 0.0)


def with_spikes(result, rng, source, target, shards_of, factor):
    def block_of(dim):
        return (jnp.arange(result.shape[dim]) // (result.shape[dim] // shards_of)).reshape((-1,) + (1,) * (result.ndim - 1 - dim))

    one_side = jax.random.permutation(rng, shards_of)[block_of(target)]
    far = (block_of(target) + shards_of // 2) % shards_of
    return jnp.where((block_of(source) == one_side) | (block_of(source) == far), factor * result, result)


def block_levels(stream_key, extent, cuts, low, top_value):
    level, own = 1.0, jax.random.fold_in(stream_key, 6)
    for dim, blocks in cuts:
        draws = jnp.exp(jax.random.uniform(jax.random.fold_in(own, dim), (blocks,), jnp.float32, low / len(cuts), top_value / len(cuts)))
        level = level * jnp.repeat(draws, extent[dim] // blocks).reshape([-1 if axis == dim else 1 for axis in range(len(extent))])
    return level


def gaussian(stream_key, shape, width, most, pieces=(), kind=jnp.bfloat16):
    entries = jax.random.normal(stream_key, shape, jnp.float32) * width
    if len(pieces) > 0:
        entries = block_levels(stream_key, shape, pieces, -0.22, 0.18) * entries
    return jnp.clip(entries, min=-most, max=most).astype(kind)


def noise_with(stream_key, shape, width, most, cuts, heavy, kind=jnp.bfloat16):
    entries = width * jax.random.normal(stream_key, shape, jnp.float32)
    if cuts:
        entries = entries * block_levels(stream_key, shape, cuts, -0.22, 0.18)
    return jnp.clip(with_spikes(entries, jax.random.fold_in(stream_key, 3), *heavy), -most, most).astype(kind)


def setup_inputs(seed: int = 0) -> dict:
    seeds = jax.random.split(jax.random.key(seed), 8)
    x_in = gaussian(seeds[0], (SEQUENCE_LENGTH, HEADS * HEAD_DIM), 1.0, 6.0, ((0, 32), (1, 16)))
    grad_out = gaussian(seeds[1], (SEQUENCE_LENGTH, HEADS * HEAD_DIM), 1.0, 6.0, ((0, 32), (1, 16)))
    step_size = draw_step_size(jax.random.fold_in(seeds[7], 71), 0)
    log_decay = draw_log_decay(jax.random.fold_in(seeds[7], 71), 0)
    b_proj = gaussian(seeds[4], (GROUPS * STATE, SEQUENCE_LENGTH), STATE ** -0.5, 0.375, ((0, 16), (1, 32)))
    c_proj = gaussian(seeds[5], (GROUPS * STATE, SEQUENCE_LENGTH), STATE ** -0.5, 0.375, ((0, 16), (1, 32)))
    w_in = noise_with(seeds[6], (HEADS * HEAD_DIM, D), D ** -0.5, 0.125, ((0, 16),), (0, 1, 16, 2.0))
    return {"x_in": x_in, "grad_out": grad_out, "step_size": step_size, "log_decay": log_decay, "b_proj": b_proj, "c_proj": c_proj, "w_in": w_in}


def rounded(value):
    return lax.optimization_barrier(value.astype(jnp.bfloat16)).astype(jnp.float32)


def reference(x_in, grad_out, step_size, log_decay, b_proj, c_proj, w_in):
    head_count = step_size.shape[0]
    per_group = 2 * HEADS_DEV
    highest = lax.Precision.HIGHEST
    block_x = x_in.reshape(N_CONTEXT, TOK_DEV, head_count, HEAD_DIM)
    block_dy = grad_out.reshape(N_CONTEXT, TOK_DEV, head_count, HEAD_DIM)
    block_dt = step_size.reshape(head_count, N_CONTEXT, TOK_DEV).transpose(1, 0, 2)
    block_cum = jnp.cumsum(log_decay.reshape(head_count, N_CONTEXT, TOK_DEV), axis=2).transpose(1, 0, 2)
    block_b = b_proj.reshape(GROUPS, STATE, N_CONTEXT, TOK_DEV).transpose(2, 0, 1, 3)
    block_c = c_proj.reshape(GROUPS, STATE, N_CONTEXT, TOK_DEV).transpose(2, 0, 1, 3)

    def ends(inputs):
        x_blk, dy_blk, dt_blk, cum_blk, b_blk, c_blk = inputs
        head_b = jnp.repeat(b_blk, per_group, axis=0).astype(jnp.float32)
        head_c = jnp.repeat(c_blk, per_group, axis=0).astype(jnp.float32)
        weighted_x = rounded((dt_blk * jnp.exp(cum_blk[:, -1:] - cum_blk)).T[:, :, None] * x_blk)
        finals = jnp.einsum("thp,hnt->hpn", weighted_x, head_b)
        weighted_dy = rounded(jnp.exp(cum_blk).T[:, :, None] * dy_blk)
        reach = jnp.einsum("thp,hnt->hpn", weighted_dy, head_c)
        return finals, reach, jnp.exp(cum_blk[:, -1])

    finals, reach, decays = lax.map(ends, (block_x, block_dy, block_dt, block_cum, block_b, block_c))

    def carry_on(state, block_item):
        term, factor = block_item
        return state * factor[:, None, None] + term, state

    start_state = jnp.zeros((head_count, HEAD_DIM, STATE), jnp.float32)
    _, state_in = lax.scan(carry_on, start_state, (finals, decays))
    _, grad_state = lax.scan(carry_on, start_state, (reach, decays), reverse=True)

    def grads(inputs):
        x_blk, dy_blk, dt_blk, cum_blk, b_blk, c_blk, s_in, g_out = inputs
        position = jnp.arange(TOK_DEV)
        causal = position[None, :] >= position[:, None]
        pair_decay = jnp.exp(jnp.where(causal[None], cum_blk[:, None, :] - cum_blk[:, :, None], -jnp.inf))
        x_wide = x_blk.astype(jnp.float32)
        dy_wide = dy_blk.astype(jnp.float32)
        intersection = jnp.einsum("thp,shp->hts", x_wide, dy_wide)
        mixing = rounded(pair_decay * intersection * dt_blk[:, :, None])
        pair_score = jnp.einsum("gnt,gns->gts", b_blk.astype(jnp.float32), c_blk.astype(jnp.float32))
        kernel = rounded(pair_decay * jnp.repeat(pair_score, per_group, axis=0))
        head_b = jnp.repeat(b_blk, per_group, axis=0).astype(jnp.float32)
        head_c = jnp.repeat(c_blk, per_group, axis=0).astype(jnp.float32)
        to_end = jnp.exp(cum_blk[:, -1:] - cum_blk)
        from_start = jnp.exp(cum_blk)
        local_dx = jnp.einsum("hts,shp->thp", kernel, dy_wide)
        carried = jnp.einsum("hnt,hpn->thp", head_b, g_out, precision=highest)
        grad_x = (dt_blk.T[:, :, None] * (local_dx + to_end.T[:, :, None] * carried)).astype(jnp.bfloat16)
        b_terms = jnp.einsum("hts,hns->hnt", mixing, head_c) + jnp.einsum(
            "thp,hpn->hnt", (dt_blk * to_end).T[:, :, None] * x_wide, g_out, precision=highest)
        c_terms = jnp.einsum("hts,hnt->hns", mixing, head_b) + jnp.einsum(
            "thp,hpn->hnt", from_start.T[:, :, None] * dy_wide, s_in, precision=highest)
        part_b = b_terms.reshape(N_TENSOR, HEADS_DEV, STATE, TOK_DEV).sum(axis=1).astype(jnp.bfloat16)
        part_c = c_terms.reshape(N_TENSOR, HEADS_DEV, STATE, TOK_DEV).sum(axis=1).astype(jnp.bfloat16)
        return grad_x.reshape(TOK_DEV, head_count * HEAD_DIM), part_b, part_c

    grad_x, part_b, part_c = lax.map(
        grads, (block_x, block_dy, block_dt, block_cum, block_b, block_c, state_in, grad_state))

    def pair_total(parts):
        paired = parts.reshape(N_CONTEXT, GROUPS, 2, STATE, TOK_DEV).astype(jnp.float32)
        summed_pair = (paired[:, :, 0] + paired[:, :, 1]).astype(jnp.bfloat16)
        return summed_pair.transpose(1, 2, 0, 3).reshape(GROUPS * STATE, N_CONTEXT * TOK_DEV)

    grad_x = grad_x.reshape(N_CONTEXT * TOK_DEV, head_count * HEAD_DIM)
    share = head_count * HEAD_DIM // N_TENSOR

    def add_device(running_sum, device):
        x_part = lax.dynamic_slice_in_dim(grad_x, device * share, share, 1)
        w_part = lax.dynamic_slice_in_dim(w_in, device * share, share, 0)
        return running_sum + rounded(jnp.dot(x_part, w_part, preferred_element_type=jnp.float32)), None

    summed, _ = lax.scan(add_device, jnp.zeros((N_CONTEXT * TOK_DEV, D), jnp.float32),
                         jnp.arange(N_TENSOR, dtype=jnp.int32))
    return summed.T.astype(jnp.bfloat16), pair_total(part_b), pair_total(part_c)
```

```python
import jax
import jax.numpy as jnp
from jax import lax
from jax.experimental import pallas as pl
from jax.experimental.pallas import tpu as pltpu
from jax.sharding import Mesh, PartitionSpec as P

CONTEXT = ("z", "yl", "core")
TENSOR = ("x", "yh")
F32 = jnp.float32
BF16 = jnp.bfloat16
HEADS = 8
WIDTH = 64
TOKENS = 256
STATE = 256
COLS = HEADS * WIDTH
BLOCKS = 32
LINES = STATE // BLOCKS


def call(body, outs, scratch=(), smem=0, flops=0):
    vmem = pl.BlockSpec(memory_space=pltpu.VMEM)
    scalar = pl.BlockSpec(memory_space=pltpu.SMEM)

    def run(*args):
        return pl.pallas_call(
            body,
            out_shape=[jax.ShapeDtypeStruct(s, d) for s, d in outs],
            in_specs=[scalar] * smem + [vmem] * (len(args) - smem),
            out_specs=[vmem] * len(outs),
            scratch_shapes=list(scratch),
            compiler_params=pltpu.CompilerParams(vmem_limit_bytes=40 * 1024 * 1024),
            cost_estimate=pl.CostEstimate(flops=flops, bytes_accessed=2**20, transcendentals=0),
        )(*args)

    return run


def iota(shape, dim):
    return lax.broadcasted_iota(jnp.int32, shape, dim)


def dot(a, b, ca, cb):
    return lax.dot_general(a, b, (((ca,), (cb,)), ((), ())), preferred_element_type=F32)


def split3(v):
    hi = v.astype(BF16).astype(F32)
    mid = (v - hi).astype(BF16).astype(F32)
    low = (v - hi - mid).astype(BF16).astype(F32)
    return hi, mid, low


def pair(cols, at, lane):
    return jnp.where(lane < WIDTH, cols[:, at : at + 1], cols[:, at + 1 : at + 2])


def pair_decay(run, cols, h):
    diff = run[h : h + 1, :] - cols[:, h : h + 1]
    causal = iota((TOKENS, TOKENS), 1) >= iota((TOKENS, TOKENS), 0)
    return jnp.exp(jnp.where(causal, diff, -jnp.inf))


def local_body(x_ref, dy_ref, dt_ref, ld_ref, wx_ref, wdy_ref, ms_ref, run_ref, cols_ref, ext_ref):
    tri = jnp.where(iota((TOKENS, TOKENS), 0) <= iota((TOKENS, TOKENS), 1), 1.0, 0.0).astype(BF16)
    parts = jnp.concatenate(split3(ld_ref[...]), axis=0).astype(BF16)
    sums = dot(parts, tri, 1, 0)
    run = sums[:HEADS] + sums[HEADS : 2 * HEADS] + sums[2 * HEADS :]
    run_ref[...] = run
    dt = dt_ref[...]
    end = run[:, TOKENS - 1 :]
    fwd = dt * jnp.exp(end - run)
    start = jnp.exp(run)
    stack = jnp.concatenate(
        [run, dt, fwd, start, jnp.zeros((128 - 4 * HEADS, TOKENS), F32)], axis=0
    )
    cols = stack.T
    cols_ref[...] = cols

    hi, mid, low = split3(jnp.exp(end))
    lane8, row8 = iota((HEADS, 128), 1), iota((HEADS, 128), 0)
    spread = jnp.where(lane8 == row8, hi, 0.0)
    spread = spread + jnp.where(lane8 == row8 + HEADS, mid, 0.0)
    spread = spread + jnp.where(lane8 == row8 + 2 * HEADS, low, 0.0)
    ext_ref[...] = jnp.sum(spread, axis=0, keepdims=True)

    lane = iota((TOKENS, 128), 1)
    total = jnp.zeros((TOKENS, TOKENS), F32)
    for i in range(HEADS // 2):
        at = slice(128 * i, 128 * (i + 1))
        xp, dyp = x_ref[:, at], dy_ref[:, at]
        wx_ref[:, at] = (pair(cols, 2 * HEADS + 2 * i, lane) * xp.astype(F32)).astype(BF16)
        wdy_ref[:, at] = (pair(cols, 3 * HEADS + 2 * i, lane) * dyp.astype(F32)).astype(BF16)
        for k in range(2):
            h = 2 * i + k
            own = (lane < WIDTH) if k == 0 else (lane >= WIDTH)
            inter = dot(jnp.where(own, xp, jnp.zeros_like(xp)), dyp, 1, 1)
            decay = pair_decay(run, cols, h)
            mixing = (decay * inter * cols[:, HEADS + h : HEADS + h + 1]).astype(BF16)
            total = total + mixing.astype(F32)
    ms_ref[...] = total.astype(BF16)


def ends_body(parity_ref, b_ref, c_ref, bc_ref, wx_ref, wdy_ref, ext_ref, bf_ref, cf_ref, send_ref):
    half = STATE // 2
    mine = pl.multiple_of(parity_ref[0] * half, half)
    other = pl.multiple_of((1 - parity_ref[0]) * half, half)
    bf_ref[pl.ds(mine, half), :] = b_ref[...]
    bf_ref[pl.ds(other, half), :] = bc_ref[:half, :]
    cf_ref[pl.ds(mine, half), :] = c_ref[...]
    cf_ref[pl.ds(other, half), :] = bc_ref[half:, :]
    send_ref[:, :COLS] = dot(bf_ref[...], wx_ref[...], 1, 0).astype(BF16)
    send_ref[:, COLS : 2 * COLS] = dot(cf_ref[...], wdy_ref[...], 1, 0).astype(BF16)
    send_ref[:, 2 * COLS :] = jnp.broadcast_to(ext_ref[...], (STATE, 128)).astype(BF16)


def scan_body(got_ref, out_ref, decay_ref):
    source, target = iota((128, COLS), 0), iota((128, COLS), 1)
    expand = (source < 3 * HEADS) & (source % HEADS == target // WIDTH)
    expand = jnp.where(expand, 1.0, 0.0).astype(BF16)
    decay_ref[...] = dot(got_ref[:, 2 * COLS :], expand, 1, 0)
    two = 2 * LINES
    state = jnp.zeros((LINES, COLS), F32)
    for c in range(BLOCKS // 2):
        at = slice(c * two, (c + 1) * two)
        term, decay = got_ref[at, :COLS].astype(F32), decay_ref[at, :]
        after = state * decay[:LINES] + term[:LINES]
        out_ref[at, :COLS] = jnp.concatenate([state, after], axis=0).astype(BF16)
        state = after * decay[LINES:] + term[LINES:]
    state = jnp.zeros((LINES, COLS), F32)
    for c in range(BLOCKS // 2 - 1, -1, -1):
        at = slice(c * two, (c + 1) * two)
        term, decay = got_ref[at, COLS : 2 * COLS].astype(F32), decay_ref[at, :]
        before = state * decay[LINES:] + term[LINES:]
        out_ref[at, COLS:] = jnp.concatenate([before, state], axis=0).astype(BF16)
        state = before * decay[:LINES] + term[:LINES]


def grad_x_body(dy_ref, bf_ref, cf_ref, run_ref, cols_ref, states_ref, gx_ref):
    run, cols = run_ref[...], cols_ref[...]
    bt = bf_ref[...].T
    score = dot(bt, cf_ref[...], 1, 0)
    lane = iota((TOKENS, 128), 1)
    for i in range(HEADS // 2):
        at = slice(128 * i, 128 * (i + 1))
        dyp = dy_ref[:, at]
        local = []
        for k in range(2):
            kernel = (pair_decay(run, cols, 2 * i + k) * score).astype(BF16)
            local.append(dot(kernel, dyp, 1, 0))
        local = jnp.where(lane < WIDTH, local[0], local[1])
        carried = dot(bt, states_ref[:, COLS + 128 * i : COLS + 128 * (i + 1)], 1, 0)
        dt, fwd = pair(cols, HEADS + 2 * i, lane), pair(cols, 2 * HEADS + 2 * i, lane)
        gx_ref[:, at] = (dt * local + fwd * carried).astype(BF16)


def grad_bc_body(parity_ref, bf_ref, cf_ref, ms_ref, wx_ref, wdy_ref, states_ref, mine_ref, send_ref, pb_ref, pc_ref):
    half = STATE // 2
    pb_ref[...] = (
        dot(cf_ref[...], ms_ref[...], 1, 1) + dot(states_ref[:, COLS:], wx_ref[...], 1, 1)
    ).astype(BF16)
    pc_ref[...] = (
        dot(bf_ref[...], ms_ref[...], 1, 0) + dot(states_ref[:, :COLS], wdy_ref[...], 1, 1)
    ).astype(BF16)
    mine = pl.multiple_of(parity_ref[0] * half, half)
    other = pl.multiple_of((1 - parity_ref[0]) * half, half)
    mine_ref[:half, :] = pb_ref[pl.ds(mine, half), :]
    mine_ref[half:, :] = pc_ref[pl.ds(mine, half), :]
    send_ref[:half, :] = pb_ref[pl.ds(other, half), :]
    send_ref[half:, :] = pc_ref[pl.ds(other, half), :]


def add_bc_body(mine_ref, got_ref, gb_ref, gc_ref):
    half = STATE // 2
    total = (mine_ref[...].astype(F32) + got_ref[...].astype(F32)).astype(BF16)
    gb_ref[...] = total[:half]
    gc_ref[...] = total[half:]


def project_body(gx_ref, w_ref, out_ref):
    tile = out_ref.shape[2]
    for j in range(out_ref.shape[0]):
        out_ref[j] = dot(gx_ref[...], w_ref[:, j * tile : (j + 1) * tile], 1, 0).astype(BF16)


def add_x_body(got_ref, out_ref):
    total = got_ref[0].astype(F32)
    for k in range(1, got_ref.shape[0]):
        total = total + got_ref[k].astype(F32)
    out_ref[...] = total.astype(BF16)


def add_y_body(got_ref, out_ref):
    total = got_ref[0].astype(F32)
    for k in range(1, got_ref.shape[0]):
        total = total + got_ref[k].astype(F32)
    out_ref[...] = total.T.astype(BF16)


def per_device(x_in, grad_out, step_size, log_decay, b_proj, c_proj, w_in):
    parity = (lax.axis_index("yh") % 2).reshape(1)
    flip = [(i, i ^ 1) for i in range(lax.axis_size("yh"))]
    bc = lax.ppermute(jnp.concatenate([b_proj, c_proj], axis=0), "yh", flip)

    square = (TOKENS, TOKENS)
    wide = (TOKENS, COLS)
    wx, wdy, mixed, run, cols, ext = call(
        local_body,
        [(wide, BF16), (wide, BF16), (square, BF16), ((HEADS, TOKENS), F32), ((TOKENS, 128), F32), ((1, 128), F32)],
        flops=10**9,
    )(x_in, grad_out, step_size, log_decay)
    b_full, c_full, send = call(
        ends_body,
        [(square, BF16), (square, BF16), ((STATE, 2 * COLS + 128), BF16)],
        smem=1,
        flops=10**9,
    )(parity, b_proj, c_proj, bc, wx, wdy, ext)
    got = lax.all_to_all(send, CONTEXT, 0, 0, tiled=True)
    (scanned,) = call(
        scan_body, [((STATE, 2 * COLS), BF16)], [pltpu.VMEM((STATE, COLS), F32)], flops=10**9
    )(got)
    states = lax.all_to_all(scanned, CONTEXT, 0, 0, tiled=True)

    (gx,) = call(grad_x_body, [(wide, BF16)], flops=10**9)(grad_out, b_full, c_full, run, cols, states)
    (partial,) = call(project_body, [((16, TOKENS, TOKENS), BF16)], flops=10**9)(gx, w_in)
    over_x = lax.all_to_all(partial, "x", 0, 0, tiled=True)

    mine, send_bc = call(
        grad_bc_body,
        [(square, BF16), (square, BF16)],
        [pltpu.VMEM(square, BF16), pltpu.VMEM(square, BF16)],
        smem=1,
        flops=10**9,
    )(parity, b_full, c_full, mixed, wx, wdy, states)
    got_bc = lax.ppermute(send_bc, "yh", flip)

    (summed,) = call(add_x_body, [((4, TOKENS, TOKENS), BF16)], flops=10**8)(
        over_x.reshape(4, 4, TOKENS, TOKENS)
    )
    over_y = lax.all_to_all(summed, "yh", 0, 0, tiled=True)
    (grad_input,) = call(add_y_body, [(square, BF16)], flops=10**8)(over_y)
    grad_b, grad_c = call(add_bc_body, [((128, TOKENS), BF16)] * 2, flops=10**8)(mine, got_bc)
    return grad_input, grad_b, grad_c


def solution(mesh):
    fine = Mesh(mesh.devices.reshape(8, 2, 2, 4, 4), CONTEXT + TENSOR)
    by_token, by_head = P(CONTEXT, TENSOR), P(TENSOR, CONTEXT)
    return jax.shard_map(
        per_device,
        mesh=fine,
        in_specs=(by_token, by_token, by_head, by_head, by_head, by_head, P(TENSOR, None)),
        out_specs=(by_head, by_head, by_head),
        check_vma=False,
    )
```

```python
import jax
import jax.numpy as jnp
from jax import lax
from jax.experimental import pallas as pl
from jax.experimental.pallas import tpu as pltpu
from jax.sharding import Mesh, PartitionSpec as P

CONTEXT = ("z", "yl", "core")
TENSOR = ("x", "yh")
F32 = jnp.float32
BF16 = jnp.bfloat16
HEADS = 8
WIDTH = 64
TOKENS = 256
STATE = 256
COLS = HEADS * WIDTH
HALF = STATE // 2
BLOCKS = 32
LINES = STATE // BLOCKS


SPACES = {
    "s": pl.BlockSpec(memory_space=pltpu.SMEM),
    "v": pl.BlockSpec(memory_space=pltpu.VMEM),
    "V": pl.BlockSpec(memory_space=pltpu.VMEM),
    "b": pl.BlockSpec(memory_space=pltpu.VMEM),
    "h": pl.BlockSpec(memory_space=pltpu.HBM),
    "a": pl.BlockSpec(memory_space=pl.ANY),
}
PLACES = {"h": pltpu.HBM, "b": pltpu.HBM, "V": pltpu.VMEM}
PASS_FLOPS = 2 * 10**10
LIMIT = 16 * 1024 * 1024


def call(body, spaces, outs, scratch=(), copies=0, out_spaces="", flops=10**9):
    run = pl.pallas_call(
        body,
        out_shape=[
            PLACES[k](s, d) if k in PLACES else jax.ShapeDtypeStruct(s, d)
            for (s, d), k in zip(outs, out_spaces or "V" * len(outs))
        ],
        in_specs=[SPACES[k] for k in spaces],
        out_specs=[SPACES[k] for k in out_spaces or "V" * len(outs)],
        scratch_shapes=[pltpu.VMEM(s, d) for s, d in scratch]
        + ([pltpu.SemaphoreType.DMA((copies,))] if copies else []),
        compiler_params=pltpu.CompilerParams(vmem_limit_bytes=LIMIT),
        cost_estimate=pl.CostEstimate(flops=flops, bytes_accessed=2**20, transcendentals=0),
    )

    def pinned(*args):
        return run(
            *(pltpu.with_memory_space_constraint(a, PLACES[k]) if k in PLACES else a for a, k in zip(args, spaces))
        )

    return pinned


def fetch(pairs, sems):
    copies = [pltpu.make_async_copy(a, b, sems.at[i]) for i, (a, b) in enumerate(pairs)]
    for copy in copies:
        copy.start()
    return copies


def iota(shape, dim):
    return lax.broadcasted_iota(jnp.int32, shape, dim)


def dot(a, b, ca, cb):
    return lax.dot_general(a, b, (((ca,), (cb,)), ((), ())), preferred_element_type=F32)


def split3(v):
    hi = v.astype(BF16).astype(F32)
    mid = (v - hi).astype(BF16).astype(F32)
    low = (v - hi - mid).astype(BF16).astype(F32)
    return hi, mid, low


def pair(cols, at, lane):
    return jnp.where(lane < WIDTH, cols[:, at : at + 1], cols[:, at + 1 : at + 2])


def pair_decay(run, cols, h):
    diff = run[h : h + 1, :] - cols[:, h : h + 1]
    causal = iota((TOKENS, TOKENS), 1) >= iota((TOKENS, TOKENS), 0)
    return jnp.exp(jnp.where(causal, diff, -jnp.inf))


def expanded(ext):
    source, target = iota((128, COLS), 0), iota((128, COLS), 1)
    spread = (source < 3 * HEADS) & (source % HEADS == target // WIDTH)
    return dot(ext, jnp.where(spread, 1.0, 0.0).astype(BF16), 1, 0)


def local_body(
    where_ref, x_hbm, dy_hbm, dt_hbm, ld_hbm, b_hbm, c_hbm, w_hbm,
    wx_ref, wdy_ref, ms_ref, run_ref, cols_ref, ext_ref, b_ref, c_ref, w1_hbm, w3_hbm, w2_hbm,
    x_ref, dy_ref, dt_ref, ld_ref, w_ref, sems,
):
    rows, share = w1_hbm.shape
    down = pl.ds(pl.multiple_of(where_ref[0] * rows, rows), rows)
    pieces = [(ld_hbm, ld_ref), (dt_hbm, dt_ref), (x_hbm, x_ref), (dy_hbm, dy_ref), (b_hbm, b_ref), (c_hbm, c_ref)]
    for i, ahead in enumerate((1, 3, 2)):
        across = pl.ds(pl.multiple_of(lax.rem(where_ref[1] + ahead, 4) * share, share), share)
        pieces.append((w_hbm.at[down, across], w_ref.at[i]))
    late = fetch(pieces, sems)
    late[0].wait()
    tri = jnp.where(iota((TOKENS, TOKENS), 0) <= iota((TOKENS, TOKENS), 1), 1.0, 0.0).astype(BF16)
    parts = jnp.concatenate(split3(ld_ref[...]), axis=0).astype(BF16)
    sums = dot(parts, tri, 1, 0)
    run = sums[:HEADS] + sums[HEADS : 2 * HEADS] + sums[2 * HEADS :]
    run_ref[...] = run
    late[1].wait()
    dt = dt_ref[...]
    end = run[:, TOKENS - 1 :]
    fwd = dt * jnp.exp(end - run)
    start = jnp.exp(run)
    stack = jnp.concatenate(
        [run, dt, fwd, start, jnp.zeros((128 - 4 * HEADS, TOKENS), F32)], axis=0
    )
    cols = stack.T
    cols_ref[...] = cols

    hi, mid, low = split3(jnp.exp(end))
    lane8, row8 = iota((HEADS, 128), 1), iota((HEADS, 128), 0)
    spread = jnp.where(lane8 == row8, hi, 0.0)
    spread = spread + jnp.where(lane8 == row8 + HEADS, mid, 0.0)
    spread = spread + jnp.where(lane8 == row8 + 2 * HEADS, low, 0.0)
    ext_ref[...] = jnp.sum(spread, axis=0, keepdims=True)

    late[2].wait()
    late[3].wait()
    lane = iota((TOKENS, 128), 1)
    total = jnp.zeros((TOKENS, TOKENS), F32)
    for i in range(HEADS // 2):
        if i == HEADS // 2 - 2:
            for copy in late[4:]:
                copy.wait()
            out = [pltpu.make_async_copy(w_ref.at[k], w, sems.at[9 + k]) for k, w in enumerate((w1_hbm, w3_hbm, w2_hbm))]
            for copy in out:
                copy.start()
        at = slice(128 * i, 128 * (i + 1))
        xp, dyp = x_ref[:, at], dy_ref[:, at]
        wx_ref[:, at] = (pair(cols, 2 * HEADS + 2 * i, lane) * xp.astype(F32)).astype(BF16)
        wdy_ref[:, at] = (pair(cols, 3 * HEADS + 2 * i, lane) * dyp.astype(F32)).astype(BF16)
        for k in range(2):
            h = 2 * i + k
            own = (lane < WIDTH) if k == 0 else (lane >= WIDTH)
            inter = dot(jnp.where(own, xp, jnp.zeros_like(xp)), dyp, 1, 1)
            decay = pair_decay(run, cols, h)
            mixing = (decay * inter * cols[:, HEADS + h : HEADS + h + 1]).astype(BF16)
            total = total + mixing.astype(F32)
    ms_ref[...] = total.astype(BF16)
    for copy in out:
        copy.wait()


def whole(own_ref, other):
    return jnp.concatenate([own_ref[...], other], axis=0)


def ends_body(b_ref, c_ref, bc_ref, wx_ref, wdy_ref, ext_ref, send_ref):
    send_ref[:, :COLS] = dot(whole(b_ref, bc_ref[:HALF]), wx_ref[...], 1, 0).astype(BF16)
    send_ref[:, COLS : 2 * COLS] = dot(whole(c_ref, bc_ref[HALF:]), wdy_ref[...], 1, 0).astype(BF16)
    send_ref[:, 2 * COLS :] = jnp.broadcast_to(ext_ref[...], (STATE, 128)).astype(BF16)


def scan_body(got_ref, out_ref, decay_ref):
    decay_ref[...] = expanded(got_ref[:, 2 * COLS :])
    two = 2 * LINES
    state = jnp.zeros((LINES, COLS), F32)
    for c in range(BLOCKS // 2):
        at = slice(c * two, (c + 1) * two)
        term, decay = got_ref[at, :COLS].astype(F32), decay_ref[at, :]
        after = state * decay[:LINES] + term[:LINES]
        out_ref[at, :COLS] = jnp.concatenate([state, after], axis=0).astype(BF16)
        state = after * decay[LINES:] + term[LINES:]
    state = jnp.zeros((LINES, COLS), F32)
    for c in range(BLOCKS // 2 - 1, -1, -1):
        at = slice(c * two, (c + 1) * two)
        term, decay = got_ref[at, COLS : 2 * COLS].astype(F32), decay_ref[at, :]
        before = state * decay[LINES:] + term[LINES:]
        out_ref[at, COLS:] = jnp.concatenate([before, state], axis=0).astype(BF16)
        state = before * decay[:LINES] + term[:LINES]


def local_x_body(dy_ref, b_ref, c_ref, bc_ref, run_ref, cols_ref, loc_ref, bt_ref):
    run, cols = run_ref[...], cols_ref[...]
    bt = whole(b_ref, bc_ref[:HALF]).T
    bt_ref[...] = bt
    score = dot(bt, whole(c_ref, bc_ref[HALF:]), 1, 0)
    lane = iota((TOKENS, 128), 1)
    for i in range(HEADS // 2):
        at = slice(128 * i, 128 * (i + 1))
        dyp = dy_ref[:, at]
        local = []
        for k in range(2):
            kernel = (pair_decay(run, cols, 2 * i + k) * score).astype(BF16)
            local.append(dot(kernel, dyp, 1, 0))
        loc_ref[:, at] = pair(cols, HEADS + 2 * i, lane) * jnp.where(lane < WIDTH, local[0], local[1])


def grad_x_body(bt_hbm, cols_hbm, loc_hbm, states_ref, out_ref, bt_ref, cols_ref, loc_ref, gx_ref, sems):
    count = out_ref.shape[0]
    early = fetch([(bt_hbm, bt_ref), (cols_hbm, cols_ref), (loc_hbm, loc_ref)], sems)
    lane = iota((TOKENS, 128), 1)
    early[0].wait()
    carried = dot(bt_ref[...], states_ref[:, COLS:], 1, 0)
    early[1].wait()
    early[2].wait()
    late = []
    for i in range(HEADS // 2):
        at = slice(128 * i, 128 * (i + 1))
        fwd = pair(cols_ref[...], 2 * HEADS + 2 * i, lane)
        gx_ref[:, at] = (loc_ref[:, at] + fwd * carried[:, at]).astype(BF16)
        if i % 2 == 1:
            done = slice(128 * (i - 1), 128 * (i + 1))
            for k in range(count):
                copy = pltpu.make_async_copy(gx_ref.at[:, done], out_ref.at[k, :, done], sems.at[3 + len(late)])
                copy.start()
                late.append(copy)
    for copy in late:
        copy.wait()


def grad_bc_body(b_ref, c_ref, bc_ref, ms_ref, wx_ref, wdy_ref, states_ref, keep_ref, send_ref):
    b_full, c_full = whole(b_ref, bc_ref[:HALF]), whole(c_ref, bc_ref[HALF:])
    part_b = (dot(c_full, ms_ref[...], 1, 1) + dot(states_ref[:, COLS:], wx_ref[...], 1, 1)).astype(BF16)
    part_c = (dot(b_full, ms_ref[...], 1, 0) + dot(states_ref[:, :COLS], wdy_ref[...], 1, 1)).astype(BF16)
    keep_ref[:HALF, :] = part_b[:HALF]
    keep_ref[HALF:, :] = part_c[:HALF]
    send_ref[:HALF, :] = part_b[HALF:]
    send_ref[HALF:, :] = part_c[HALF:]


def add_bc_body(mine_ref, got_ref, gb_ref, gc_ref):
    half = STATE // 2
    total = (mine_ref[...].astype(F32) + got_ref[...].astype(F32)).astype(BF16)
    gb_ref[...] = total[:half]
    gc_ref[...] = total[half:]


def pass_body(*refs):
    pass


def passed(*arrays):
    anywhere = [SPACES["a"]] * len(arrays)
    return pl.pallas_call(
        pass_body,
        out_shape=[jax.ShapeDtypeStruct(v.shape, v.dtype) for v in arrays],
        in_specs=anywhere,
        out_specs=anywhere,
        input_output_aliases={i: i for i in range(len(arrays))},
        cost_estimate=pl.CostEstimate(flops=PASS_FLOPS, bytes_accessed=2**20, transcendentals=0),
    )(*arrays)


def load_body(where_ref, w_hbm, *refs):
    *pieces, out_ref, sems = refs
    core, here, share, half = where_ref[0], where_ref[1], out_ref.shape[1], COLS // 2
    pairs = [(w_hbm.at[:, pl.ds(pl.multiple_of(here * share, share), share)], out_ref.at[:COLS, :])]
    for i, piece in enumerate(pieces):
        side = core if i < 3 else 1 - core
        start = pl.multiple_of((i % 3 + 1) * COLS + side * half, half)
        pairs.append((piece, out_ref.at[pl.ds(start, half), :]))
    for copy in fetch(pairs, sems):
        copy.wait()


def project_body(where_ref, gx_ref, w_ref, out_ref, tiles_ref, sems):
    tile, count = out_ref.shape[2], gx_ref.shape[0]
    gx = [gx_ref[lax.rem(where_ref[1] + count - i, count)] for i in range(count)]
    gx = jnp.concatenate(gx, axis=1)
    late = []
    for j in range(out_ref.shape[0]):
        tiles_ref[j] = dot(gx, w_ref[:, j * tile : (j + 1) * tile], 1, 0).astype(BF16)
        copy = pltpu.make_async_copy(tiles_ref.at[j], out_ref.at[j], sems.at[j])
        copy.start()
        late.append(copy)
    for copy in late:
        copy.wait()


def add_y_body(got_ref, out_ref):
    total = got_ref[0].astype(F32)
    for k in range(1, got_ref.shape[0]):
        total = total + got_ref[k].astype(F32)
    out_ref[...] = total.T.astype(BF16)


def per_device(x_in, grad_out, step_size, log_decay, b_proj, c_proj, w_in):
    hold = lax.optimization_barrier
    core, x_index = lax.axis_index("core"), lax.axis_index("x")
    flip = [(i, i ^ 1) for i in range(lax.axis_size("yh"))]
    half = w_in.shape[0] // 2
    share = w_in.shape[1] // 4
    square, wide, own_half = (TOKENS, TOKENS), (TOKENS, COLS), (HALF, TOKENS)

    def ahead_on_x(shard, ahead):
        return lax.ppermute(shard, "x", [(i, (i + ahead) % 4) for i in range(4)])

    def other_core(shard):
        return lax.ppermute(shard, "core", [(0, 1), (1, 0)])

    where = jnp.stack([core, x_index])
    bc = lax.ppermute(jnp.concatenate([b_proj, c_proj], axis=0), "yh", flip)
    wx, wdy, mixed, run, cols, ext, b_own, c_own, w_next, w_prev, w_far = call(
        local_body,
        "shhhhhhh",
        [(wide, BF16), (wide, BF16), (square, BF16), ((HEADS, TOKENS), F32), ((TOKENS, 128), F32), ((1, 128), F32)]
        + [(own_half, BF16)] * 2
        + [((half, share), BF16)] * 3,
        [(wide, BF16), (wide, BF16), ((HEADS, TOKENS), F32), ((HEADS, TOKENS), F32), ((3, half, share), BF16)],
        copies=12,
        out_spaces="vvbvbvvvhhh",
    )(where, x_in, grad_out, step_size, log_decay, b_proj, c_proj, w_in)
    (send,) = call(ends_body, "vvvvvv", [((STATE, 2 * COLS + 128), BF16)], out_spaces="v")(
        b_own, c_own, bc, wx, wdy, ext
    )

    terms = lax.all_to_all(send, CONTEXT, 0, 0, tiled=True)
    w_next, w_prev, w_far, bc, _ = hold((w_next, w_prev, w_far, bc, send))
    w_prev, w_next, w_far = ahead_on_x(w_next, 1), ahead_on_x(w_prev, 3), ahead_on_x(w_far, 2)
    local_x, b_rows = call(local_x_body, "vbbvvb", [(wide, F32), (square, BF16)], out_spaces="bb")(
        grad_out, b_proj, c_proj, bc, run, cols
    )
    (scanned,) = call(scan_body, "v", [((STATE, 2 * COLS), BF16)], [((STATE, COLS), F32)], out_spaces="v")(terms)
    states = lax.all_to_all(scanned, CONTEXT, 0, 0, tiled=True)
    w_prev, w_far, w_next, _ = hold((w_prev, w_far, w_next, scanned))
    w_mine = passed(w_prev, w_far, w_next)
    w_theirs = [other_core(w) for w in w_mine]
    states, w_mine, w_theirs = hold((states, w_mine, w_theirs))

    (gx,) = call(
        grad_x_body,
        "hhhv",
        [((4, *wide), BF16)],
        [(square, BF16), ((TOKENS, 128), F32), (wide, F32), (wide, BF16)],
        copies=11,
        out_spaces="h",
    )(b_rows, cols, local_x, states)
    gx_x = lax.all_to_all(gx, "x", 0, 0, tiled=True)
    states, w_mine, _ = hold((states, w_mine, gx))
    keep_bc, send_bc = call(grad_bc_body, "bbvbvvv", [(square, BF16), (square, BF16)], out_spaces="vv")(
        b_proj, c_proj, bc, mixed, wx, wdy, states
    )
    got_bc = lax.ppermute(send_bc, "yh", flip)
    (w_here,) = call(load_body, "shhhhhhh", [((4 * COLS, share), BF16)], copies=7, out_spaces="V")(
        where, w_in, *w_mine, *w_theirs
    )
    gx_x, got_bc, w_here = hold((gx_x, got_bc, w_here))

    (partial,) = call(
        project_body, "svV", [((4, *square), BF16)], [((4, *square), BF16)], copies=4, out_spaces="h"
    )(where, gx_x, w_here)
    over_y = lax.all_to_all(partial, "yh", 0, 0, tiled=True)
    (grad_input,) = call(add_y_body, "v", [(square, BF16)], out_spaces="v")(over_y)
    grad_b, grad_c = call(add_bc_body, "vv", [(own_half, BF16), (own_half, BF16)], out_spaces="vv")(keep_bc, got_bc)
    return grad_input, grad_b, grad_c


def solution(mesh):
    fine = Mesh(mesh.devices.reshape(8, 2, 2, 4, 4), CONTEXT + TENSOR)
    by_token, by_head = P(CONTEXT, TENSOR), P(TENSOR, CONTEXT)
    return jax.shard_map(
        per_device,
        mesh=fine,
        in_specs=(by_token, by_token, by_head, by_head, by_head, by_head, P(TENSOR, None)),
        out_specs=(by_head, by_head, by_head),
        check_vma=False,
    )
```

```python
import jax
import jax.numpy as jnp
from jax import lax
from jax.experimental import pallas as pl
from jax.experimental.pallas import tpu as pltpu
from jax.sharding import Mesh, PartitionSpec as P

CONTEXT = ("z", "yl", "core")
TENSOR = ("x", "yh")
F32 = jnp.float32
BF16 = jnp.bfloat16
HEADS = 8
WIDTH = 64
TOKENS = 256
STATE = 256
COLS = HEADS * WIDTH
HALF = STATE // 2
BLOCKS = 32
LINES = STATE // BLOCKS


SPACES = {
    "s": pl.BlockSpec(memory_space=pltpu.SMEM),
    "v": pl.BlockSpec(memory_space=pltpu.VMEM),
    "V": pl.BlockSpec(memory_space=pltpu.VMEM),
    "b": pl.BlockSpec(memory_space=pltpu.VMEM),
    "h": pl.BlockSpec(memory_space=pltpu.HBM),
    "a": pl.BlockSpec(memory_space=pl.ANY),
}
PLACES = {"h": pltpu.HBM, "b": pltpu.HBM, "V": pltpu.VMEM}
ADD_FLOPS = 10 * 10**9
PASS_FLOPS = 4 * 10**9
LIMIT = 16 * 1024 * 1024


def call(body, spaces, outs, scratch=(), copies=0, out_spaces="", flops=10**9):
    run = pl.pallas_call(
        body,
        out_shape=[
            PLACES[k](s, d) if k in PLACES else jax.ShapeDtypeStruct(s, d)
            for (s, d), k in zip(outs, out_spaces or "V" * len(outs))
        ],
        in_specs=[SPACES[k] for k in spaces],
        out_specs=[SPACES[k] for k in out_spaces or "V" * len(outs)],
        scratch_shapes=[pltpu.VMEM(s, d) for s, d in scratch]
        + ([pltpu.SemaphoreType.DMA((copies,))] if copies else []),
        compiler_params=pltpu.CompilerParams(vmem_limit_bytes=LIMIT),
        cost_estimate=pl.CostEstimate(flops=flops, bytes_accessed=2**20, transcendentals=0),
    )

    def pinned(*args):
        return run(
            *(pltpu.with_memory_space_constraint(a, PLACES[k]) if k in PLACES else a for a, k in zip(args, spaces))
        )

    return pinned


def fetch(pairs, sems):
    copies = [pltpu.make_async_copy(a, b, sems.at[i]) for i, (a, b) in enumerate(pairs)]
    for copy in copies:
        copy.start()
    return copies


def iota(shape, dim):
    return lax.broadcasted_iota(jnp.int32, shape, dim)


def dot(a, b, ca, cb):
    return lax.dot_general(a, b, (((ca,), (cb,)), ((), ())), preferred_element_type=F32)


def split3(v):
    hi = v.astype(BF16).astype(F32)
    mid = (v - hi).astype(BF16).astype(F32)
    low = (v - hi - mid).astype(BF16).astype(F32)
    return hi, mid, low


def pair(cols, at, lane):
    return jnp.where(lane < WIDTH, cols[:, at : at + 1], cols[:, at + 1 : at + 2])


def pair_decay(run, cols, h):
    diff = run[h : h + 1, :] - cols[:, h : h + 1]
    causal = iota((TOKENS, TOKENS), 1) >= iota((TOKENS, TOKENS), 0)
    return jnp.exp(jnp.where(causal, diff, -jnp.inf))


def expanded(ext):
    source, target = iota((128, COLS), 0), iota((128, COLS), 1)
    spread = (source < 3 * HEADS) & (source % HEADS == target // WIDTH)
    return dot(ext, jnp.where(spread, 1.0, 0.0).astype(BF16), 1, 0)


def local_body(
    where_ref, x_hbm, dy_hbm, dt_hbm, ld_hbm, b_hbm, c_hbm, w_hbm,
    wx_ref, wdy_ref, ms_ref, run_ref, cols_ref, ext_ref, b_ref, c_ref, w1_hbm, w3_hbm, w2_hbm, wx_hbm, wdy_hbm,
    x_ref, dy_ref, dt_ref, ld_ref, w_ref, sems,
):
    rows, share = w1_hbm.shape
    down = pl.ds(pl.multiple_of(where_ref[0] * rows, rows), rows)
    pieces = [(ld_hbm, ld_ref), (dt_hbm, dt_ref), (x_hbm, x_ref), (dy_hbm, dy_ref), (b_hbm, b_ref), (c_hbm, c_ref)]
    for i, ahead in enumerate((1, 3, 2)):
        across = pl.ds(pl.multiple_of(lax.rem(where_ref[1] + ahead, 4) * share, share), share)
        pieces.append((w_hbm.at[down, across], w_ref.at[i]))
    late = fetch(pieces, sems)
    late[0].wait()
    tri = jnp.where(iota((TOKENS, TOKENS), 0) <= iota((TOKENS, TOKENS), 1), 1.0, 0.0).astype(BF16)
    parts = jnp.concatenate(split3(ld_ref[...]), axis=0).astype(BF16)
    sums = dot(parts, tri, 1, 0)
    run = sums[:HEADS] + sums[HEADS : 2 * HEADS] + sums[2 * HEADS :]
    run_ref[...] = run
    late[1].wait()
    dt = dt_ref[...]
    end = run[:, TOKENS - 1 :]
    fwd = dt * jnp.exp(end - run)
    start = jnp.exp(run)
    stack = jnp.concatenate(
        [run, dt, fwd, start, jnp.zeros((128 - 4 * HEADS, TOKENS), F32)], axis=0
    )
    cols = stack.T
    cols_ref[...] = cols

    hi, mid, low = split3(jnp.exp(end))
    lane8, row8 = iota((HEADS, 128), 1), iota((HEADS, 128), 0)
    spread = jnp.where(lane8 == row8, hi, 0.0)
    spread = spread + jnp.where(lane8 == row8 + HEADS, mid, 0.0)
    spread = spread + jnp.where(lane8 == row8 + 2 * HEADS, low, 0.0)
    ext_ref[...] = jnp.sum(spread, axis=0, keepdims=True)

    late[2].wait()
    late[3].wait()
    lane = iota((TOKENS, 128), 1)
    total = jnp.zeros((TOKENS, TOKENS), F32)
    for i in range(HEADS // 2):
        if i == HEADS // 2 - 2:
            for copy in late[4:]:
                copy.wait()
            out = [pltpu.make_async_copy(w_ref.at[k], w, sems.at[9 + k]) for k, w in enumerate((w1_hbm, w3_hbm, w2_hbm))]
            for copy in out:
                copy.start()
        at = slice(128 * i, 128 * (i + 1))
        xp, dyp = x_ref[:, at], dy_ref[:, at]
        wx_ref[:, at] = (pair(cols, 2 * HEADS + 2 * i, lane) * xp.astype(F32)).astype(BF16)
        wdy_ref[:, at] = (pair(cols, 3 * HEADS + 2 * i, lane) * dyp.astype(F32)).astype(BF16)
        for k in range(2):
            h = 2 * i + k
            own = (lane < WIDTH) if k == 0 else (lane >= WIDTH)
            inter = dot(jnp.where(own, xp, jnp.zeros_like(xp)), dyp, 1, 1)
            decay = pair_decay(run, cols, h)
            mixing = (decay * inter * cols[:, HEADS + h : HEADS + h + 1]).astype(BF16)
            total = total + mixing.astype(F32)
    ms_ref[...] = total.astype(BF16)
    for i, (a, b) in enumerate(((wx_ref, wx_hbm), (wdy_ref, wdy_hbm))):
        out.append(pltpu.make_async_copy(a, b, sems.at[12 + i]))
        out[-1].start()
    for copy in out:
        copy.wait()


def whole(own_ref, other):
    return jnp.concatenate([own_ref[...], other], axis=0)


def ends_body(b_ref, c_ref, other_b, other_c, wx_ref, wdy_ref, ext_ref, send_hbm, send_ref, sems):
    parts = [slice(0, COLS), slice(COLS, 2 * COLS + 128)]
    copies = [pltpu.make_async_copy(send_ref.at[:, at], send_hbm.at[:, at], sems.at[i]) for i, at in enumerate(parts)]
    send_ref[:, :COLS] = dot(whole(b_ref, other_b[...]), wx_ref[...], 1, 0).astype(BF16)
    copies[0].start()
    send_ref[:, COLS : 2 * COLS] = dot(whole(c_ref, other_c[...]), wdy_ref[...], 1, 0).astype(BF16)
    send_ref[:, 2 * COLS :] = jnp.broadcast_to(ext_ref[...], (STATE, 128)).astype(BF16)
    copies[1].start()
    for copy in copies:
        copy.wait()


def scan_body(got_ref, out_hbm, out_ref, decay_ref, sems):
    halves = [slice(0, COLS), slice(COLS, 2 * COLS)]
    copies = [pltpu.make_async_copy(out_ref.at[:, at], out_hbm.at[:, at], sems.at[i]) for i, at in enumerate(halves)]
    decay_ref[...] = expanded(got_ref[:, 2 * COLS :])
    two = 2 * LINES
    state = jnp.zeros((LINES, COLS), F32)
    for c in range(BLOCKS // 2):
        at = slice(c * two, (c + 1) * two)
        term, decay = got_ref[at, :COLS].astype(F32), decay_ref[at, :]
        after = state * decay[:LINES] + term[:LINES]
        out_ref[at, :COLS] = jnp.concatenate([state, after], axis=0).astype(BF16)
        state = after * decay[LINES:] + term[LINES:]
    copies[0].start()
    state = jnp.zeros((LINES, COLS), F32)
    for c in range(BLOCKS // 2 - 1, -1, -1):
        at = slice(c * two, (c + 1) * two)
        term, decay = got_ref[at, COLS : 2 * COLS].astype(F32), decay_ref[at, :]
        before = state * decay[LINES:] + term[LINES:]
        out_ref[at, COLS:] = jnp.concatenate([before, state], axis=0).astype(BF16)
        state = before * decay[:LINES] + term[:LINES]
    copies[1].start()
    for copy in copies:
        copy.wait()


def local_x_body(dy_ref, b_ref, c_ref, other_b, other_c, run_ref, cols_ref, loc_ref, bt_ref):
    run, cols = run_ref[...], cols_ref[...]
    bt = whole(b_ref, other_b[...]).T
    bt_ref[...] = bt
    score = dot(bt, whole(c_ref, other_c[...]), 1, 0)
    lane = iota((TOKENS, 128), 1)
    for i in range(HEADS // 2):
        at = slice(128 * i, 128 * (i + 1))
        dyp = dy_ref[:, at]
        local = []
        for k in range(2):
            kernel = (pair_decay(run, cols, 2 * i + k) * score).astype(BF16)
            local.append(dot(kernel, dyp, 1, 0))
        loc_ref[:, at] = pair(cols, HEADS + 2 * i, lane) * jnp.where(lane < WIDTH, local[0], local[1])


def grad_x_body(bt_hbm, cols_hbm, loc_hbm, states_ref, gx_ref, bt_ref, cols_ref, loc_ref, sems):
    early = fetch([(bt_hbm, bt_ref), (cols_hbm, cols_ref), (loc_hbm, loc_ref)], sems)
    lane = iota((TOKENS, 128), 1)
    early[0].wait()
    carried = dot(bt_ref[...], states_ref[:, COLS:], 1, 0)
    early[1].wait()
    early[2].wait()
    for i in range(HEADS // 2):
        at = slice(128 * i, 128 * (i + 1))
        fwd = pair(cols_ref[...], 2 * HEADS + 2 * i, lane)
        gx_ref[:, at] = (loc_ref[:, at] + fwd * carried[:, at]).astype(BF16)


def grad_bc_body(b_ref, c_ref, other_b, other_c, ms_ref, wx_ref, wdy_ref, states_ref, keep_ref, send_ref):
    b_full, c_full = whole(b_ref, other_b[...]), whole(c_ref, other_c[...])
    part_b = (dot(c_full, ms_ref[...], 1, 1) + dot(states_ref[:, COLS:], wx_ref[...], 1, 1)).astype(BF16)
    part_c = (dot(b_full, ms_ref[...], 1, 0) + dot(states_ref[:, :COLS], wdy_ref[...], 1, 1)).astype(BF16)
    keep_ref[:HALF, :] = part_b[:HALF]
    keep_ref[HALF:, :] = part_c[:HALF]
    send_ref[:HALF, :] = part_b[HALF:]
    send_ref[HALF:, :] = part_c[HALF:]


def add_bc_body(mine_ref, got_ref, gb_ref, gc_ref):
    half = STATE // 2
    total = (mine_ref[...].astype(F32) + got_ref[...].astype(F32)).astype(BF16)
    gb_ref[...] = total[:half]
    gc_ref[...] = total[half:]


def pass_body(*refs):
    pass


def passed(*arrays):
    anywhere = [SPACES["a"]] * len(arrays)
    return pl.pallas_call(
        pass_body,
        out_shape=[jax.ShapeDtypeStruct(v.shape, v.dtype) for v in arrays],
        in_specs=anywhere,
        out_specs=anywhere,
        input_output_aliases={i: i for i in range(len(arrays))},
        compiler_params=pltpu.CompilerParams(vmem_limit_bytes=LIMIT),
        cost_estimate=pl.CostEstimate(flops=PASS_FLOPS, bytes_accessed=2**20, transcendentals=0),
    )(*arrays)


def load_body(where_ref, w_hbm, *refs):
    *pieces, w_ref, sems = refs
    core, here, share, half = where_ref[0], where_ref[1], w_ref.shape[1], COLS // 2
    pairs = [(w_hbm.at[:, pl.ds(pl.multiple_of(here * share, share), share)], w_ref.at[:COLS, :])]
    for i, piece in enumerate(pieces):
        side = core if i < 3 else 1 - core
        start = pl.multiple_of((i % 3 + 1) * COLS + side * half, half)
        pairs.append((piece, w_ref.at[pl.ds(start, half), :]))
    for copy in fetch(pairs, sems):
        copy.wait()


def project_body(w_ref, *refs):
    *gx_refs, out_hbm, tiles_ref, sems = refs
    tile = out_hbm.shape[2]
    late = []
    for j in range(out_hbm.shape[0]):
        total = jnp.zeros((TOKENS, tile), F32)
        for k, gx_ref in enumerate(gx_refs):
            total = total + dot(gx_ref[...], w_ref[k * COLS : (k + 1) * COLS, j * tile : (j + 1) * tile], 1, 0)
        tiles_ref[j] = total.astype(BF16)
        copy = pltpu.make_async_copy(tiles_ref.at[j], out_hbm.at[j], sems.at[j])
        copy.start()
        late.append(copy)
    for copy in late:
        copy.wait()


def add_y_body(got_ref, out_ref):
    total = got_ref[0].astype(F32)
    for k in range(1, got_ref.shape[0]):
        total = total + got_ref[k].astype(F32)
    out_ref[...] = total.T.astype(BF16)


def per_device(x_in, grad_out, step_size, log_decay, b_proj, c_proj, w_in):
    hold = lax.optimization_barrier
    core, x_index = lax.axis_index("core"), lax.axis_index("x")
    flip = [(i, i ^ 1) for i in range(lax.axis_size("yh"))]
    half = w_in.shape[0] // 2
    share = w_in.shape[1] // 4
    square, wide, own_half = (TOKENS, TOKENS), (TOKENS, COLS), (HALF, TOKENS)

    def ahead_on_x(shard, ahead):
        return lax.ppermute(shard, "x", [(i, (i + ahead) % 4) for i in range(4)])

    def other_core(shard):
        return lax.ppermute(shard, "core", [(0, 1), (1, 0)])

    where = jnp.stack([core, x_index])
    bc = lax.ppermute(b_proj, "yh", flip), lax.ppermute(c_proj, "yh", flip)
    wx, wdy, mixed, run, cols, ext, b_own, c_own, w_next, w_prev, w_far, wx_late, wdy_late = call(
        local_body,
        "shhhhhhh",
        [(wide, BF16), (wide, BF16), (square, BF16), ((HEADS, TOKENS), F32), ((TOKENS, 128), F32), ((1, 128), F32)]
        + [(own_half, BF16)] * 2
        + [((half, share), BF16)] * 3
        + [(wide, BF16)] * 2,
        [(wide, BF16), (wide, BF16), ((HEADS, TOKENS), F32), ((HEADS, TOKENS), F32), ((3, half, share), BF16)],
        copies=14,
        out_spaces="vvbvbvvvhhhhh",
    )(where, x_in, grad_out, step_size, log_decay, b_proj, c_proj, w_in)
    ends = ((STATE, 2 * COLS + 128), BF16)
    (send,) = call(ends_body, "vvvvvvv", [ends], [ends], copies=2, out_spaces="h")(b_own, c_own, *bc, wx, wdy, ext)

    terms = lax.all_to_all(send, CONTEXT, 0, 0, tiled=True)
    w_next, w_prev, w_far, bc, _ = hold((w_next, w_prev, w_far, bc, send))
    w_prev, w_next, w_far = ahead_on_x(w_next, 1), ahead_on_x(w_prev, 3), ahead_on_x(w_far, 2)
    local_x, b_rows = call(local_x_body, "vbbvvvb", [(wide, F32), (square, BF16)], out_spaces="bb")(
        grad_out, b_proj, c_proj, *bc, run, cols
    )
    terms, local_x, b_rows = hold((terms, local_x, b_rows))
    both = ((STATE, 2 * COLS), BF16)
    (scanned,) = call(scan_body, "v", [both], [both, ((STATE, COLS), F32)], copies=2, out_spaces="h")(terms)
    states = lax.all_to_all(scanned, CONTEXT, 0, 0, tiled=True)
    w_prev, w_far, w_next, _ = hold((w_prev, w_far, w_next, scanned))
    w_mine = passed(w_prev, w_far, w_next)
    w_theirs = [other_core(w) for w in w_mine]
    states, w_mine, w_theirs = hold((states, w_mine, w_theirs))

    (gx,) = call(
        grad_x_body, "hhhv", [(wide, BF16)], [(square, BF16), ((TOKENS, 128), F32), (wide, F32)], copies=3, out_spaces="v"
    )(b_rows, cols, local_x, states)
    gx_far = ahead_on_x(gx, 2)
    gx_prev, gx_next = ahead_on_x(gx, 1), ahead_on_x(gx, 3)
    states, w_mine, _ = hold((states, w_mine, gx))
    keep_bc, send_bc = call(grad_bc_body, "bbvvbbbv", [(square, BF16), (square, BF16)], out_spaces="vv")(
        b_proj, c_proj, *bc, mixed, wx_late, wdy_late, states
    )
    got_bc = lax.ppermute(send_bc, "yh", flip)
    (w_here,) = call(load_body, "shhhhhhh", [((4 * COLS, share), BF16)], copies=7, out_spaces="V")(
        where, w_in, *w_mine, *w_theirs
    )
    gx_prev, gx_far, gx_next, w_here = hold((gx_prev, gx_far, gx_next, w_here))

    four = ((4, *square), BF16)
    (partial,) = call(project_body, "Vvvvv", [four], [four], copies=4, out_spaces="h")(
        w_here, gx, gx_prev, gx_far, gx_next
    )
    over_y = lax.all_to_all(partial, "yh", 0, 0, tiled=True)
    (grad_input,) = call(add_y_body, "v", [(square, BF16)], out_spaces="v")(over_y)
    grad_b, grad_c = call(
        add_bc_body, "vv", [(own_half, BF16), (own_half, BF16)], out_spaces="vv", flops=ADD_FLOPS
    )(keep_bc, got_bc)
    return grad_input, grad_b, grad_c


def solution(mesh):
    fine = Mesh(mesh.devices.reshape(8, 2, 2, 4, 4), CONTEXT + TENSOR)
    by_token, by_head = P(CONTEXT, TENSOR), P(TENSOR, CONTEXT)
    return jax.shard_map(
        per_device,
        mesh=fine,
        in_specs=(by_token, by_token, by_head, by_head, by_head, by_head, P(TENSOR, None)),
        out_specs=(by_head, by_head, by_head),
        check_vma=False,
    )
```

```python
import jax
import jax.numpy as jnp
from jax import lax
from jax.experimental import pallas as pl
from jax.experimental.pallas import tpu as pltpu
from jax.sharding import Mesh, PartitionSpec as P

CONTEXT = ("z", "yl", "core")
TENSOR = ("x", "yh")
F32 = jnp.float32
BF16 = jnp.bfloat16
HEADS = 8
WIDTH = 64
TOKENS = 256
STATE = 256
COLS = HEADS * WIDTH
HALF = STATE // 2
BLOCKS = 32
LINES = STATE // BLOCKS


SPACES = {
    "s": pl.BlockSpec(memory_space=pltpu.SMEM),
    "v": pl.BlockSpec(memory_space=pltpu.VMEM),
    "V": pl.BlockSpec(memory_space=pltpu.VMEM),
    "b": pl.BlockSpec(memory_space=pltpu.VMEM),
    "h": pl.BlockSpec(memory_space=pltpu.HBM),
    "a": pl.BlockSpec(memory_space=pl.ANY),
}
PLACES = {"h": pltpu.HBM, "b": pltpu.HBM, "V": pltpu.VMEM}
ADD_FLOPS = 10 * 10**9
PASS_FLOPS = 4 * 10**9
LIMIT = 16 * 1024 * 1024


def call(body, spaces, outs, scratch=(), copies=0, out_spaces="", flops=10**9):
    run = pl.pallas_call(
        body,
        out_shape=[
            PLACES[k](s, d) if k in PLACES else jax.ShapeDtypeStruct(s, d)
            for (s, d), k in zip(outs, out_spaces or "V" * len(outs))
        ],
        in_specs=[SPACES[k] for k in spaces],
        out_specs=[SPACES[k] for k in out_spaces or "V" * len(outs)],
        scratch_shapes=[pltpu.VMEM(s, d) for s, d in scratch]
        + ([pltpu.SemaphoreType.DMA((copies,))] if copies else []),
        compiler_params=pltpu.CompilerParams(vmem_limit_bytes=LIMIT),
        cost_estimate=pl.CostEstimate(flops=flops, bytes_accessed=2**20, transcendentals=0),
    )

    def pinned(*args):
        return run(
            *(pltpu.with_memory_space_constraint(a, PLACES[k]) if k in PLACES else a for a, k in zip(args, spaces))
        )

    return pinned


def fetch(pairs, sems):
    copies = [pltpu.make_async_copy(a, b, sems.at[i]) for i, (a, b) in enumerate(pairs)]
    for copy in copies:
        copy.start()
    return copies


def iota(shape, dim):
    return lax.broadcasted_iota(jnp.int32, shape, dim)


def dot(a, b, ca, cb):
    return lax.dot_general(a, b, (((ca,), (cb,)), ((), ())), preferred_element_type=F32)


def split3(v):
    hi = v.astype(BF16).astype(F32)
    mid = (v - hi).astype(BF16).astype(F32)
    low = (v - hi - mid).astype(BF16).astype(F32)
    return hi, mid, low


def pair(cols, at, lane):
    return jnp.where(lane < WIDTH, cols[:, at : at + 1], cols[:, at + 1 : at + 2])


def pair_decay(run, cols, h):
    diff = run[h : h + 1, :] - cols[:, h : h + 1]
    causal = iota((TOKENS, TOKENS), 1) >= iota((TOKENS, TOKENS), 0)
    return jnp.exp(jnp.where(causal, diff, -jnp.inf))


def expanded(ext):
    source, target = iota((128, COLS), 0), iota((128, COLS), 1)
    spread = (source < 3 * HEADS) & (source % HEADS == target // WIDTH)
    return dot(ext, jnp.where(spread, 1.0, 0.0).astype(BF16), 1, 0)


def weights_body(
    where_ref, x_hbm, dy_hbm, dt_hbm, ld_hbm, b_hbm, c_hbm, w_hbm,
    wx_ref, wdy_ref, run_ref, cols_hbm, ext_ref, b_ref, c_ref, w1_hbm, w3_hbm, w2_hbm, wx_hbm, wdy_hbm, fwd_hbm,
    x_ref, dy_ref, dt_ref, ld_ref, cols_ref, w_ref, fwd_ref, sems,
):
    rows, share = w1_hbm.shape
    down = pl.ds(pl.multiple_of(where_ref[0] * rows, rows), rows)
    pieces = [(ld_hbm, ld_ref), (dt_hbm, dt_ref), (x_hbm, x_ref), (dy_hbm, dy_ref), (b_hbm, b_ref), (c_hbm, c_ref)]
    for i, ahead in enumerate((1, 3, 2)):
        across = pl.ds(pl.multiple_of(lax.rem(where_ref[1] + ahead, 4) * share, share), share)
        pieces.append((w_hbm.at[down, across], w_ref.at[i]))
    late = fetch(pieces, sems)
    out = []

    def put(source, target):
        out.append(pltpu.make_async_copy(source, target, sems.at[len(pieces) + len(out)]))
        out[-1].start()

    late[0].wait()
    tri = jnp.where(iota((TOKENS, TOKENS), 0) <= iota((TOKENS, TOKENS), 1), 1.0, 0.0).astype(BF16)
    parts = jnp.concatenate(split3(ld_ref[...]), axis=0).astype(BF16)
    sums = dot(parts, tri, 1, 0)
    run = sums[:HEADS] + sums[HEADS : 2 * HEADS] + sums[2 * HEADS :]
    run_ref[...] = run
    late[1].wait()
    dt = dt_ref[...]
    end = run[:, TOKENS - 1 :]
    fwd = dt * jnp.exp(end - run)
    fwd_ref[...] = fwd
    put(fwd_ref, fwd_hbm)
    start = jnp.exp(run)
    stack = jnp.concatenate(
        [run, dt, fwd, start, jnp.zeros((128 - 4 * HEADS, TOKENS), F32)], axis=0
    )
    cols = stack.T
    cols_ref[...] = cols
    put(cols_ref, cols_hbm)

    hi, mid, low = split3(jnp.exp(end))
    lane8, row8 = iota((HEADS, 128), 1), iota((HEADS, 128), 0)
    spread = jnp.where(lane8 == row8, hi, 0.0)
    spread = spread + jnp.where(lane8 == row8 + HEADS, mid, 0.0)
    spread = spread + jnp.where(lane8 == row8 + 2 * HEADS, low, 0.0)
    ext_ref[...] = jnp.sum(spread, axis=0, keepdims=True)

    lane = iota((TOKENS, 128), 1)
    late[2].wait()
    for i in range(HEADS // 2):
        at = slice(128 * i, 128 * (i + 1))
        wx_ref[:, at] = (pair(cols, 2 * HEADS + 2 * i, lane) * x_ref[:, at].astype(F32)).astype(BF16)
    put(wx_ref, wx_hbm)
    late[3].wait()
    for i in range(HEADS // 2):
        at = slice(128 * i, 128 * (i + 1))
        wdy_ref[:, at] = (pair(cols, 3 * HEADS + 2 * i, lane) * dy_ref[:, at].astype(F32)).astype(BF16)
    put(wdy_ref, wdy_hbm)
    for copy in late[4:]:
        copy.wait()
    for k, w in enumerate((w1_hbm, w3_hbm, w2_hbm)):
        put(w_ref.at[k], w)
    for copy in out:
        copy.wait()


def whole(own_ref, other):
    return jnp.concatenate([own_ref[...], other], axis=0)


def ends_body(b_ref, c_ref, other_b, other_c, wx_ref, wdy_ref, ext_ref, send_hbm, send_ref, sems):
    parts = [slice(0, COLS), slice(COLS, 2 * COLS + 128)]
    copies = [pltpu.make_async_copy(send_ref.at[:, at], send_hbm.at[:, at], sems.at[i]) for i, at in enumerate(parts)]
    send_ref[:, :COLS] = dot(whole(b_ref, other_b[...]), wx_ref[...], 1, 0).astype(BF16)
    copies[0].start()
    send_ref[:, COLS : 2 * COLS] = dot(whole(c_ref, other_c[...]), wdy_ref[...], 1, 0).astype(BF16)
    send_ref[:, 2 * COLS :] = jnp.broadcast_to(ext_ref[...], (STATE, 128)).astype(BF16)
    copies[1].start()
    for copy in copies:
        copy.wait()


def scan_body(got_ref, out_hbm, out_ref, decay_ref, sems):
    halves = [slice(0, COLS), slice(COLS, 2 * COLS)]
    copies = [pltpu.make_async_copy(out_ref.at[:, at], out_hbm.at[:, at], sems.at[i]) for i, at in enumerate(halves)]
    decay_ref[...] = expanded(got_ref[:, 2 * COLS :])
    two = 2 * LINES
    state = jnp.zeros((LINES, COLS), F32)
    for c in range(BLOCKS // 2):
        at = slice(c * two, (c + 1) * two)
        term, decay = got_ref[at, :COLS].astype(F32), decay_ref[at, :]
        after = state * decay[:LINES] + term[:LINES]
        out_ref[at, :COLS] = jnp.concatenate([state, after], axis=0).astype(BF16)
        state = after * decay[LINES:] + term[LINES:]
    copies[0].start()
    state = jnp.zeros((LINES, COLS), F32)
    for c in range(BLOCKS // 2 - 1, -1, -1):
        at = slice(c * two, (c + 1) * two)
        term, decay = got_ref[at, COLS : 2 * COLS].astype(F32), decay_ref[at, :]
        before = state * decay[LINES:] + term[LINES:]
        out_ref[at, COLS:] = jnp.concatenate([before, state], axis=0).astype(BF16)
        state = before * decay[:LINES] + term[:LINES]
    copies[1].start()
    for copy in copies:
        copy.wait()


def local_x_body(x_ref, dy_ref, b_ref, c_ref, other_b, other_c, run_ref, cols_ref, loc_ref, bt_ref, ms_ref):
    run, cols = run_ref[...], cols_ref[...]
    bt = whole(b_ref, other_b[...]).T
    bt_ref[...] = bt
    score = dot(bt, whole(c_ref, other_c[...]), 1, 0)
    lane = iota((TOKENS, 128), 1)
    total = jnp.zeros((TOKENS, TOKENS), F32)
    for i in range(HEADS // 2):
        at = slice(128 * i, 128 * (i + 1))
        xp, dyp = x_ref[:, at], dy_ref[:, at]
        local = []
        for k in range(2):
            h = 2 * i + k
            own = (lane < WIDTH) if k == 0 else (lane >= WIDTH)
            decay = pair_decay(run, cols, h)
            inter = dot(jnp.where(own, xp, jnp.zeros_like(xp)), dyp, 1, 1)
            mixing = (decay * inter * cols[:, HEADS + h : HEADS + h + 1]).astype(BF16)
            total = total + mixing.astype(F32)
            local.append(dot((decay * score).astype(BF16), dyp, 1, 0))
        local = pair(cols, HEADS + 2 * i, lane) * jnp.where(lane < WIDTH, local[0], local[1])
        loc_ref[:, at] = local.astype(BF16)
    ms_ref[...] = total.astype(BF16)


def grad_x_body(bt_hbm, fwd_hbm, loc_hbm, states_ref, gx_ref, bt_ref, fwd_ref, loc_ref, sems):
    early = fetch([(bt_hbm, bt_ref), (fwd_hbm, fwd_ref), (loc_hbm, loc_ref)], sems)
    lane = iota((TOKENS, 128), 1)
    early[1].wait()
    cols = jnp.concatenate([fwd_ref[...], jnp.zeros((128 - HEADS, TOKENS), F32)], axis=0).T
    early[0].wait()
    early[2].wait()
    for i in range(HEADS // 2):
        at = slice(128 * i, 128 * (i + 1))
        carried = dot(bt_ref[...], states_ref[:, COLS + 128 * i : COLS + 128 * (i + 1)], 1, 0)
        gx_ref[:, at] = (loc_ref[:, at].astype(F32) + pair(cols, 2 * i, lane) * carried).astype(BF16)


def grad_bc_body(b_ref, c_ref, other_b, other_c, ms_ref, wx_ref, wdy_ref, states_ref, keep_ref, send_ref):
    b_full, c_full = whole(b_ref, other_b[...]), whole(c_ref, other_c[...])
    part_b = (dot(c_full, ms_ref[...], 1, 1) + dot(states_ref[:, COLS:], wx_ref[...], 1, 1)).astype(BF16)
    part_c = (dot(b_full, ms_ref[...], 1, 0) + dot(states_ref[:, :COLS], wdy_ref[...], 1, 1)).astype(BF16)
    keep_ref[:HALF, :] = part_b[:HALF]
    keep_ref[HALF:, :] = part_c[:HALF]
    send_ref[:HALF, :] = part_b[HALF:]
    send_ref[HALF:, :] = part_c[HALF:]


def add_bc_body(mine_ref, got_ref, gb_ref, gc_ref):
    half = STATE // 2
    total = (mine_ref[...].astype(F32) + got_ref[...].astype(F32)).astype(BF16)
    gb_ref[...] = total[:half]
    gc_ref[...] = total[half:]


def pass_body(*refs):
    pass


def passed(*arrays):
    anywhere = [SPACES["a"]] * len(arrays)
    return pl.pallas_call(
        pass_body,
        out_shape=[jax.ShapeDtypeStruct(v.shape, v.dtype) for v in arrays],
        in_specs=anywhere,
        out_specs=anywhere,
        input_output_aliases={i: i for i in range(len(arrays))},
        compiler_params=pltpu.CompilerParams(vmem_limit_bytes=LIMIT),
        cost_estimate=pl.CostEstimate(flops=PASS_FLOPS, bytes_accessed=2**20, transcendentals=0),
    )(*arrays)


def load_body(where_ref, w_hbm, *refs):
    *pieces, w_ref, sems = refs
    core, here, share, half = where_ref[0], where_ref[1], w_ref.shape[1], COLS // 2
    pairs = [(w_hbm.at[:, pl.ds(pl.multiple_of(here * share, share), share)], w_ref.at[:COLS, :])]
    for i, piece in enumerate(pieces):
        side = core if i < 3 else 1 - core
        start = pl.multiple_of((i % 3 + 1) * COLS + side * half, half)
        pairs.append((piece, w_ref.at[pl.ds(start, half), :]))
    for copy in fetch(pairs, sems):
        copy.wait()


def project_body(w_ref, *refs):
    *gx_refs, out_hbm, tiles_ref, sems = refs
    tile = out_hbm.shape[2]
    late = []
    for j in range(out_hbm.shape[0]):
        total = jnp.zeros((TOKENS, tile), F32)
        for k, gx_ref in enumerate(gx_refs):
            total = total + dot(gx_ref[...], w_ref[k * COLS : (k + 1) * COLS, j * tile : (j + 1) * tile], 1, 0)
        tiles_ref[j] = total.astype(BF16)
        copy = pltpu.make_async_copy(tiles_ref.at[j], out_hbm.at[j], sems.at[j])
        copy.start()
        late.append(copy)
    for copy in late:
        copy.wait()


def add_y_body(got_ref, out_ref):
    total = got_ref[0].astype(F32)
    for k in range(1, got_ref.shape[0]):
        total = total + got_ref[k].astype(F32)
    out_ref[...] = total.T.astype(BF16)


def per_device(x_in, grad_out, step_size, log_decay, b_proj, c_proj, w_in):
    hold = lax.optimization_barrier
    core, x_index = lax.axis_index("core"), lax.axis_index("x")
    flip = [(i, i ^ 1) for i in range(lax.axis_size("yh"))]
    half = w_in.shape[0] // 2
    share = w_in.shape[1] // 4
    square, wide, own_half = (TOKENS, TOKENS), (TOKENS, COLS), (HALF, TOKENS)

    def ahead_on_x(shard, ahead):
        return lax.ppermute(shard, "x", [(i, (i + ahead) % 4) for i in range(4)])

    def other_core(shard):
        return lax.ppermute(shard, "core", [(0, 1), (1, 0)])

    where = jnp.stack([core, x_index])
    bc = lax.ppermute(b_proj, "yh", flip), lax.ppermute(c_proj, "yh", flip)
    wx, wdy, run, cols, ext, b_own, c_own, w_next, w_prev, w_far, wx_late, wdy_late, fwd = call(
        weights_body,
        "shhhhhhh",
        [(wide, BF16), (wide, BF16), ((HEADS, TOKENS), F32), ((TOKENS, 128), F32), ((1, 128), F32)]
        + [(own_half, BF16)] * 2
        + [((half, share), BF16)] * 3
        + [(wide, BF16)] * 2
        + [((HEADS, TOKENS), F32)],
        [(wide, BF16), (wide, BF16), ((HEADS, TOKENS), F32), ((HEADS, TOKENS), F32)]
        + [((TOKENS, 128), F32), ((3, half, share), BF16), ((HEADS, TOKENS), F32)],
        copies=16,
        out_spaces="vvvhvvvhhhhhh",
    )(where, x_in, grad_out, step_size, log_decay, b_proj, c_proj, w_in)
    ends = ((STATE, 2 * COLS + 128), BF16)
    (send,) = call(ends_body, "vvvvvvv", [ends], [ends], copies=2, out_spaces="h")(b_own, c_own, *bc, wx, wdy, ext)

    terms = lax.all_to_all(send, CONTEXT, 0, 0, tiled=True)
    w_next, w_prev, w_far, bc, _ = hold((w_next, w_prev, w_far, bc, send))
    w_prev, w_next, w_far = ahead_on_x(w_next, 1), ahead_on_x(w_prev, 3), ahead_on_x(w_far, 2)
    local_x, b_rows, mixed = call(
        local_x_body, "bbbbvvvb", [(wide, BF16), (square, BF16), (square, BF16)], out_spaces="bbb"
    )(x_in, grad_out, b_proj, c_proj, *bc, run, cols)
    terms, local_x, b_rows, mixed = hold((terms, local_x, b_rows, mixed))
    both = ((STATE, 2 * COLS), BF16)
    (scanned,) = call(scan_body, "v", [both], [both, ((STATE, COLS), F32)], copies=2, out_spaces="h")(terms)
    states = lax.all_to_all(scanned, CONTEXT, 0, 0, tiled=True)
    w_prev, w_far, w_next, _ = hold((w_prev, w_far, w_next, scanned))
    w_mine = passed(w_prev, w_far, w_next)
    w_theirs = [other_core(w) for w in w_mine]
    states, w_mine, w_theirs = hold((states, w_mine, w_theirs))

    (gx,) = call(
        grad_x_body, "hhhv", [(wide, BF16)], [(square, BF16), ((HEADS, TOKENS), F32), (wide, BF16)], copies=3, out_spaces="v"
    )(b_rows, fwd, local_x, states)
    gx_far = ahead_on_x(gx, 2)
    gx_prev, gx_next = ahead_on_x(gx, 1), ahead_on_x(gx, 3)
    states, w_mine, _ = hold((states, w_mine, gx))
    keep_bc, send_bc = call(grad_bc_body, "bbvvbbbv", [(square, BF16), (square, BF16)], out_spaces="vv")(
        b_proj, c_proj, *bc, mixed, wx_late, wdy_late, states
    )
    got_bc = lax.ppermute(send_bc, "yh", flip)
    (w_here,) = call(load_body, "shhhhhhh", [((4 * COLS, share), BF16)], copies=7, out_spaces="V")(
        where, w_in, *w_mine, *w_theirs
    )
    gx_prev, gx_far, gx_next, w_here = hold((gx_prev, gx_far, gx_next, w_here))

    four = ((4, *square), BF16)
    (partial,) = call(project_body, "Vvvvv", [four], [four], copies=4, out_spaces="h")(
        w_here, gx, gx_prev, gx_far, gx_next
    )
    over_y = lax.all_to_all(partial, "yh", 0, 0, tiled=True)
    (grad_input,) = call(add_y_body, "v", [(square, BF16)], out_spaces="v")(over_y)
    grad_b, grad_c = call(
        add_bc_body, "vv", [(own_half, BF16), (own_half, BF16)], out_spaces="vv", flops=ADD_FLOPS
    )(keep_bc, got_bc)
    return grad_input, grad_b, grad_c


def solution(mesh):
    fine = Mesh(mesh.devices.reshape(8, 2, 2, 4, 4), CONTEXT + TENSOR)
    by_token, by_head = P(CONTEXT, TENSOR), P(TENSOR, CONTEXT)
    return jax.shard_map(
        per_device,
        mesh=fine,
        in_specs=(by_token, by_token, by_head, by_head, by_head, by_head, P(TENSOR, None)),
        out_specs=(by_head, by_head, by_head),
        check_vma=False,
    )
```

```python
import jax
import jax.numpy as jnp
from jax import lax
from jax.experimental import pallas as pl
from jax.experimental.pallas import tpu as pltpu
from jax.sharding import Mesh, PartitionSpec as P

CONTEXT = ("z", "yl", "core")
EXCHANGE = ("yl", "z", "core")
TENSOR = ("x", "yh")
F32 = jnp.float32
BF16 = jnp.bfloat16
HEADS = 8
WIDTH = 64
TOKENS = 256
STATE = 256
COLS = HEADS * WIDTH
HALF = STATE // 2
BLOCKS = 32
LINES = STATE // BLOCKS


SPACES = {
    "s": pl.BlockSpec(memory_space=pltpu.SMEM),
    "v": pl.BlockSpec(memory_space=pltpu.VMEM),
    "V": pl.BlockSpec(memory_space=pltpu.VMEM),
    "b": pl.BlockSpec(memory_space=pltpu.VMEM),
    "h": pl.BlockSpec(memory_space=pltpu.HBM),
    "a": pl.BlockSpec(memory_space=pl.ANY),
}
PLACES = {"h": pltpu.HBM, "b": pltpu.HBM, "V": pltpu.VMEM}
ADD_FLOPS = 10 * 10**9
PASS_FLOPS = 4 * 10**9
LIMIT = 16 * 1024 * 1024


def call(body, spaces, outs, scratch=(), copies=0, out_spaces="", flops=10**9):
    run = pl.pallas_call(
        body,
        out_shape=[
            PLACES[k](s, d) if k in PLACES else jax.ShapeDtypeStruct(s, d)
            for (s, d), k in zip(outs, out_spaces or "V" * len(outs))
        ],
        in_specs=[SPACES[k] for k in spaces],
        out_specs=[SPACES[k] for k in out_spaces or "V" * len(outs)],
        scratch_shapes=[pltpu.VMEM(s, d) for s, d in scratch]
        + ([pltpu.SemaphoreType.DMA((copies,))] if copies else []),
        compiler_params=pltpu.CompilerParams(vmem_limit_bytes=LIMIT),
        cost_estimate=pl.CostEstimate(flops=flops, bytes_accessed=2**20, transcendentals=0),
    )

    def pinned(*args):
        return run(
            *(pltpu.with_memory_space_constraint(a, PLACES[k]) if k in PLACES else a for a, k in zip(args, spaces))
        )

    return pinned


def fetch(pairs, sems):
    copies = [pltpu.make_async_copy(a, b, sems.at[i]) for i, (a, b) in enumerate(pairs)]
    for copy in copies:
        copy.start()
    return copies


def iota(shape, dim):
    return lax.broadcasted_iota(jnp.int32, shape, dim)


def dot(a, b, ca, cb):
    return lax.dot_general(a, b, (((ca,), (cb,)), ((), ())), preferred_element_type=F32)


def split3(v):
    hi = v.astype(BF16).astype(F32)
    mid = (v - hi).astype(BF16).astype(F32)
    low = (v - hi - mid).astype(BF16).astype(F32)
    return hi, mid, low


def pair(cols, at, lane):
    return jnp.where(lane < WIDTH, cols[:, at : at + 1], cols[:, at + 1 : at + 2])


def pair_decay(run, cols, h):
    diff = run[h : h + 1, :] - cols[:, h : h + 1]
    causal = iota((TOKENS, TOKENS), 1) >= iota((TOKENS, TOKENS), 0)
    return jnp.exp(jnp.where(causal, diff, -jnp.inf))


def expanded(ext):
    source, target = iota((128, COLS), 0), iota((128, COLS), 1)
    spread = (source < 3 * HEADS) & (source % HEADS == target // WIDTH)
    return dot(ext, jnp.where(spread, 1.0, 0.0).astype(BF16), 1, 0)


def weights_body(
    where_ref, x_hbm, dy_hbm, dt_hbm, ld_hbm, b_hbm, c_hbm, w_hbm,
    wx_ref, wdy_ref, run_ref, cols_hbm, ext_ref, b_ref, c_ref, w1_hbm, w3_hbm, w2_hbm, wx_hbm, wdy_hbm, fwd_hbm,
    x_ref, dy_ref, dt_ref, ld_ref, cols_ref, w_ref, fwd_ref, sems,
):
    rows, share = w1_hbm.shape
    down = pl.ds(pl.multiple_of(where_ref[0] * rows, rows), rows)
    pieces = [(ld_hbm, ld_ref), (dt_hbm, dt_ref), (x_hbm, x_ref), (dy_hbm, dy_ref), (b_hbm, b_ref), (c_hbm, c_ref)]
    for i, ahead in enumerate((1, 3, 2)):
        across = pl.ds(pl.multiple_of(lax.rem(where_ref[1] + ahead, 4) * share, share), share)
        pieces.append((w_hbm.at[down, across], w_ref.at[i]))
    late = fetch(pieces, sems)
    out = []

    def put(source, target):
        out.append(pltpu.make_async_copy(source, target, sems.at[len(pieces) + len(out)]))
        out[-1].start()

    late[0].wait()
    tri = jnp.where(iota((TOKENS, TOKENS), 0) <= iota((TOKENS, TOKENS), 1), 1.0, 0.0).astype(BF16)
    parts = jnp.concatenate(split3(ld_ref[...]), axis=0).astype(BF16)
    sums = dot(parts, tri, 1, 0)
    run = sums[:HEADS] + sums[HEADS : 2 * HEADS] + sums[2 * HEADS :]
    run_ref[...] = run
    late[1].wait()
    dt = dt_ref[...]
    end = run[:, TOKENS - 1 :]
    fwd = dt * jnp.exp(end - run)
    fwd_ref[...] = fwd
    put(fwd_ref, fwd_hbm)
    start = jnp.exp(run)
    stack = jnp.concatenate(
        [run, dt, fwd, start, jnp.zeros((128 - 4 * HEADS, TOKENS), F32)], axis=0
    )
    cols = stack.T
    cols_ref[...] = cols
    put(cols_ref, cols_hbm)

    hi, mid, low = split3(jnp.exp(end))
    lane8, row8 = iota((HEADS, 128), 1), iota((HEADS, 128), 0)
    spread = jnp.where(lane8 == row8, hi, 0.0)
    spread = spread + jnp.where(lane8 == row8 + HEADS, mid, 0.0)
    spread = spread + jnp.where(lane8 == row8 + 2 * HEADS, low, 0.0)
    ext_ref[...] = jnp.sum(spread, axis=0, keepdims=True)

    lane = iota((TOKENS, 128), 1)
    late[2].wait()
    for i in range(HEADS // 2):
        at = slice(128 * i, 128 * (i + 1))
        wx_ref[:, at] = (pair(cols, 2 * HEADS + 2 * i, lane) * x_ref[:, at].astype(F32)).astype(BF16)
    put(wx_ref, wx_hbm)
    late[3].wait()
    for i in range(HEADS // 2):
        at = slice(128 * i, 128 * (i + 1))
        wdy_ref[:, at] = (pair(cols, 3 * HEADS + 2 * i, lane) * dy_ref[:, at].astype(F32)).astype(BF16)
    put(wdy_ref, wdy_hbm)
    for copy in late[4:]:
        copy.wait()
    for k, w in enumerate((w1_hbm, w3_hbm, w2_hbm)):
        put(w_ref.at[k], w)
    for copy in out:
        copy.wait()


def whole(own_ref, other):
    return jnp.concatenate([own_ref[...], other], axis=0)


def ends_body(b_ref, c_ref, other_b, other_c, wx_ref, wdy_ref, ext_ref, send_hbm, send_ref, sems):
    parts = [slice(0, COLS), slice(COLS, 2 * COLS + 128)]
    copies = [pltpu.make_async_copy(send_ref.at[:, at], send_hbm.at[:, at], sems.at[i]) for i, at in enumerate(parts)]
    send_ref[:, :COLS] = dot(whole(b_ref, other_b[...]), wx_ref[...], 1, 0).astype(BF16)
    copies[0].start()
    send_ref[:, COLS : 2 * COLS] = dot(whole(c_ref, other_c[...]), wdy_ref[...], 1, 0).astype(BF16)
    send_ref[:, 2 * COLS :] = jnp.broadcast_to(ext_ref[...], (STATE, 128)).astype(BF16)
    copies[1].start()
    for copy in copies:
        copy.wait()


def scan_body(got_ref, out_hbm, out_ref, decay_ref, sems):
    halves = [slice(0, COLS), slice(COLS, 2 * COLS)]
    copies = [pltpu.make_async_copy(out_ref.at[:, at], out_hbm.at[:, at], sems.at[i]) for i, at in enumerate(halves)]
    decay_ref[...] = expanded(got_ref[:, 2 * COLS :])
    two = 2 * LINES

    def place(chip):
        row = chip % 2 * (BLOCKS // 4) + chip // 2
        return slice(row * two, (row + 1) * two)

    state = jnp.zeros((LINES, COLS), F32)
    for c in range(BLOCKS // 2):
        at = place(c)
        term, decay = got_ref[at, :COLS].astype(F32), decay_ref[at, :]
        after = state * decay[:LINES] + term[:LINES]
        out_ref[at, :COLS] = jnp.concatenate([state, after], axis=0).astype(BF16)
        state = after * decay[LINES:] + term[LINES:]
    copies[0].start()
    state = jnp.zeros((LINES, COLS), F32)
    for c in range(BLOCKS // 2 - 1, -1, -1):
        at = place(c)
        term, decay = got_ref[at, COLS : 2 * COLS].astype(F32), decay_ref[at, :]
        before = state * decay[LINES:] + term[LINES:]
        out_ref[at, COLS:] = jnp.concatenate([before, state], axis=0).astype(BF16)
        state = before * decay[:LINES] + term[:LINES]
    copies[1].start()
    for copy in copies:
        copy.wait()


def local_x_body(x_ref, dy_ref, b_ref, c_ref, other_b, other_c, run_ref, cols_ref, loc_ref, bt_ref, ms_ref):
    run, cols = run_ref[...], cols_ref[...]
    bt = whole(b_ref, other_b[...]).T
    bt_ref[...] = bt
    score = dot(bt, whole(c_ref, other_c[...]), 1, 0)
    lane = iota((TOKENS, 128), 1)
    total = jnp.zeros((TOKENS, TOKENS), F32)
    for i in range(HEADS // 2):
        at = slice(128 * i, 128 * (i + 1))
        xp, dyp = x_ref[:, at], dy_ref[:, at]
        local = []
        for k in range(2):
            h = 2 * i + k
            own = (lane < WIDTH) if k == 0 else (lane >= WIDTH)
            decay = pair_decay(run, cols, h)
            inter = dot(jnp.where(own, xp, jnp.zeros_like(xp)), dyp, 1, 1)
            mixing = (decay * inter * cols[:, HEADS + h : HEADS + h + 1]).astype(BF16)
            total = total + mixing.astype(F32)
            local.append(dot((decay * score).astype(BF16), dyp, 1, 0))
        local = pair(cols, HEADS + 2 * i, lane) * jnp.where(lane < WIDTH, local[0], local[1])
        loc_ref[:, at] = local.astype(BF16)
    ms_ref[...] = total.astype(BF16)


def grad_x_body(bt_hbm, fwd_hbm, loc_hbm, states_ref, gx_ref, bt_ref, fwd_ref, loc_ref, sems):
    early = fetch([(bt_hbm, bt_ref), (fwd_hbm, fwd_ref), (loc_hbm, loc_ref)], sems)
    lane = iota((TOKENS, 128), 1)
    early[1].wait()
    cols = jnp.concatenate([fwd_ref[...], jnp.zeros((128 - HEADS, TOKENS), F32)], axis=0).T
    early[0].wait()
    early[2].wait()
    for i in range(HEADS // 2):
        at = slice(128 * i, 128 * (i + 1))
        carried = dot(bt_ref[...], states_ref[:, COLS + 128 * i : COLS + 128 * (i + 1)], 1, 0)
        gx_ref[:, at] = (loc_ref[:, at].astype(F32) + pair(cols, 2 * i, lane) * carried).astype(BF16)


def grad_bc_body(b_ref, c_ref, other_b, other_c, ms_ref, wx_ref, wdy_ref, states_ref, keep_ref, send_ref):
    b_full, c_full = whole(b_ref, other_b[...]), whole(c_ref, other_c[...])
    part_b = (dot(c_full, ms_ref[...], 1, 1) + dot(states_ref[:, COLS:], wx_ref[...], 1, 1)).astype(BF16)
    part_c = (dot(b_full, ms_ref[...], 1, 0) + dot(states_ref[:, :COLS], wdy_ref[...], 1, 1)).astype(BF16)
    keep_ref[:HALF, :] = part_b[:HALF]
    keep_ref[HALF:, :] = part_c[:HALF]
    send_ref[:HALF, :] = part_b[HALF:]
    send_ref[HALF:, :] = part_c[HALF:]


def add_bc_body(mine_ref, got_ref, gb_ref, gc_ref):
    half = STATE // 2
    total = (mine_ref[...].astype(F32) + got_ref[...].astype(F32)).astype(BF16)
    gb_ref[...] = total[:half]
    gc_ref[...] = total[half:]


def pass_body(*refs):
    pass


def passed(*arrays):
    anywhere = [SPACES["a"]] * len(arrays)
    return pl.pallas_call(
        pass_body,
        out_shape=[jax.ShapeDtypeStruct(v.shape, v.dtype) for v in arrays],
        in_specs=anywhere,
        out_specs=anywhere,
        input_output_aliases={i: i for i in range(len(arrays))},
        compiler_params=pltpu.CompilerParams(vmem_limit_bytes=LIMIT),
        cost_estimate=pl.CostEstimate(flops=PASS_FLOPS, bytes_accessed=2**20, transcendentals=0),
    )(*arrays)


def load_body(where_ref, w_hbm, *refs):
    *pieces, w_ref, sems = refs
    core, here, share, half = where_ref[0], where_ref[1], w_ref.shape[1], COLS // 2
    pairs = [(w_hbm.at[:, pl.ds(pl.multiple_of(here * share, share), share)], w_ref.at[:COLS, :])]
    for i, piece in enumerate(pieces):
        side = core if i < 3 else 1 - core
        start = pl.multiple_of((i % 3 + 1) * COLS + side * half, half)
        pairs.append((piece, w_ref.at[pl.ds(start, half), :]))
    for copy in fetch(pairs, sems):
        copy.wait()


def project_body(w_ref, *refs):
    *gx_refs, out_hbm, tiles_ref, sems = refs
    tile = out_hbm.shape[2]
    late = []
    for j in range(out_hbm.shape[0]):
        total = jnp.zeros((TOKENS, tile), F32)
        for k, gx_ref in enumerate(gx_refs):
            total = total + dot(gx_ref[...], w_ref[k * COLS : (k + 1) * COLS, j * tile : (j + 1) * tile], 1, 0)
        tiles_ref[j] = total.astype(BF16)
        copy = pltpu.make_async_copy(tiles_ref.at[j], out_hbm.at[j], sems.at[j])
        copy.start()
        late.append(copy)
    for copy in late:
        copy.wait()


def add_y_body(got_ref, out_ref):
    total = got_ref[0].astype(F32)
    for k in range(1, got_ref.shape[0]):
        total = total + got_ref[k].astype(F32)
    out_ref[...] = total.T.astype(BF16)


def per_device(x_in, grad_out, step_size, log_decay, b_proj, c_proj, w_in):
    hold = lax.optimization_barrier
    core, x_index = lax.axis_index("core"), lax.axis_index("x")
    flip = [(i, i ^ 1) for i in range(lax.axis_size("yh"))]
    half = w_in.shape[0] // 2
    share = w_in.shape[1] // 4
    square, wide, own_half = (TOKENS, TOKENS), (TOKENS, COLS), (HALF, TOKENS)

    def ahead_on_x(shard, ahead):
        return lax.ppermute(shard, "x", [(i, (i + ahead) % 4) for i in range(4)])

    def other_core(shard):
        return lax.ppermute(shard, "core", [(0, 1), (1, 0)])

    where = jnp.stack([core, x_index])
    bc = lax.ppermute(b_proj, "yh", flip), lax.ppermute(c_proj, "yh", flip)
    wx, wdy, run, cols, ext, b_own, c_own, w_next, w_prev, w_far, wx_late, wdy_late, fwd = call(
        weights_body,
        "shhhhhhh",
        [(wide, BF16), (wide, BF16), ((HEADS, TOKENS), F32), ((TOKENS, 128), F32), ((1, 128), F32)]
        + [(own_half, BF16)] * 2
        + [((half, share), BF16)] * 3
        + [(wide, BF16)] * 2
        + [((HEADS, TOKENS), F32)],
        [(wide, BF16), (wide, BF16), ((HEADS, TOKENS), F32), ((HEADS, TOKENS), F32)]
        + [((TOKENS, 128), F32), ((3, half, share), BF16), ((HEADS, TOKENS), F32)],
        copies=16,
        out_spaces="vvvhvvvhhhhhh",
    )(where, x_in, grad_out, step_size, log_decay, b_proj, c_proj, w_in)
    ends = ((STATE, 2 * COLS + 128), BF16)
    (send,) = call(ends_body, "vvvvvvv", [ends], [ends], copies=2, out_spaces="h")(b_own, c_own, *bc, wx, wdy, ext)

    terms = lax.all_to_all(send, EXCHANGE, 0, 0, tiled=True)
    w_next, w_prev, w_far, bc, _ = hold((w_next, w_prev, w_far, bc, send))
    w_prev, w_next, w_far = ahead_on_x(w_next, 1), ahead_on_x(w_prev, 3), ahead_on_x(w_far, 2)
    local_x, b_rows, mixed = call(
        local_x_body, "bbbbvvvb", [(wide, BF16), (square, BF16), (square, BF16)], out_spaces="bbb"
    )(x_in, grad_out, b_proj, c_proj, *bc, run, cols)
    terms, local_x, b_rows, mixed = hold((terms, local_x, b_rows, mixed))
    both = ((STATE, 2 * COLS), BF16)
    (scanned,) = call(scan_body, "v", [both], [both, ((STATE, COLS), F32)], copies=2, out_spaces="h")(terms)
    states = lax.all_to_all(scanned, EXCHANGE, 0, 0, tiled=True)
    w_prev, w_far, w_next, _ = hold((w_prev, w_far, w_next, scanned))
    w_mine = passed(w_prev, w_far, w_next)
    w_theirs = [other_core(w) for w in w_mine]
    states, w_mine, w_theirs = hold((states, w_mine, w_theirs))

    (gx,) = call(
        grad_x_body, "hhhv", [(wide, BF16)], [(square, BF16), ((HEADS, TOKENS), F32), (wide, BF16)], copies=3, out_spaces="v"
    )(b_rows, fwd, local_x, states)
    gx_far = ahead_on_x(gx, 2)
    gx_prev, gx_next = ahead_on_x(gx, 1), ahead_on_x(gx, 3)
    states, w_mine, _ = hold((states, w_mine, gx))
    keep_bc, send_bc = call(grad_bc_body, "bbvvbbbv", [(square, BF16), (square, BF16)], out_spaces="vv")(
        b_proj, c_proj, *bc, mixed, wx_late, wdy_late, states
    )
    got_bc = lax.ppermute(send_bc, "yh", flip)
    (w_here,) = call(load_body, "shhhhhhh", [((4 * COLS, share), BF16)], copies=7, out_spaces="V")(
        where, w_in, *w_mine, *w_theirs
    )
    gx_prev, gx_far, gx_next, w_here = hold((gx_prev, gx_far, gx_next, w_here))

    four = ((4, *square), BF16)
    (partial,) = call(project_body, "Vvvvv", [four], [four], copies=4, out_spaces="h")(
        w_here, gx, gx_prev, gx_far, gx_next
    )
    over_y = lax.all_to_all(partial, "yh", 0, 0, tiled=True)
    (grad_input,) = call(add_y_body, "v", [(square, BF16)], out_spaces="v")(over_y)
    grad_b, grad_c = call(
        add_bc_body, "vv", [(own_half, BF16), (own_half, BF16)], out_spaces="vv", flops=ADD_FLOPS
    )(keep_bc, got_bc)
    return grad_input, grad_b, grad_c


def solution(mesh):
    fine = Mesh(mesh.devices.reshape(8, 2, 2, 4, 4), CONTEXT + TENSOR)
    by_token, by_head = P(CONTEXT, TENSOR), P(TENSOR, CONTEXT)
    return jax.shard_map(
        per_device,
        mesh=fine,
        in_specs=(by_token, by_token, by_head, by_head, by_head, by_head, P(TENSOR, None)),
        out_specs=(by_head, by_head, by_head),
        check_vma=False,
    )
```

```python
import jax
import jax.numpy as jnp
from jax import lax
from jax.experimental import pallas as pl
from jax.experimental.pallas import tpu as pltpu
from jax.sharding import Mesh, PartitionSpec as P

CONTEXT = ("z", "yl", "core")
EXCHANGE = ("yl", "z", "core")
TENSOR = ("x", "yh")
F32 = jnp.float32
BF16 = jnp.bfloat16
HEADS = 8
WIDTH = 64
TOKENS = 256
STATE = 256
COLS = HEADS * WIDTH
HALF = STATE // 2
BLOCKS = 32
LINES = STATE // BLOCKS


SPACES = {
    "s": pl.BlockSpec(memory_space=pltpu.SMEM),
    "v": pl.BlockSpec(memory_space=pltpu.VMEM),
    "V": pl.BlockSpec(memory_space=pltpu.VMEM),
    "b": pl.BlockSpec(memory_space=pltpu.VMEM),
    "h": pl.BlockSpec(memory_space=pltpu.HBM),
    "a": pl.BlockSpec(memory_space=pl.ANY),
}
PLACES = {"h": pltpu.HBM, "b": pltpu.HBM, "V": pltpu.VMEM}
ADD_FLOPS = 10 * 10**9
PASS_FLOPS = 4 * 10**9
LIMIT = 16 * 1024 * 1024


def call(body, spaces, outs, scratch=(), copies=0, out_spaces="", flops=10**9):
    run = pl.pallas_call(
        body,
        out_shape=[
            PLACES[k](s, d) if k in PLACES else jax.ShapeDtypeStruct(s, d)
            for (s, d), k in zip(outs, out_spaces or "V" * len(outs))
        ],
        in_specs=[SPACES[k] for k in spaces],
        out_specs=[SPACES[k] for k in out_spaces or "V" * len(outs)],
        scratch_shapes=[pltpu.VMEM(s, d) for s, d in scratch]
        + ([pltpu.SemaphoreType.DMA((copies,))] if copies else []),
        compiler_params=pltpu.CompilerParams(vmem_limit_bytes=LIMIT),
        cost_estimate=pl.CostEstimate(flops=flops, bytes_accessed=2**20, transcendentals=0),
    )

    def pinned(*args):
        return run(
            *(pltpu.with_memory_space_constraint(a, PLACES[k]) if k in PLACES else a for a, k in zip(args, spaces))
        )

    return pinned


def fetch(pairs, sems):
    copies = [pltpu.make_async_copy(a, b, sems.at[i]) for i, (a, b) in enumerate(pairs)]
    for copy in copies:
        copy.start()
    return copies


def iota(shape, dim):
    return lax.broadcasted_iota(jnp.int32, shape, dim)


def dot(a, b, ca, cb):
    return lax.dot_general(a, b, (((ca,), (cb,)), ((), ())), preferred_element_type=F32)


def split3(v):
    hi = v.astype(BF16).astype(F32)
    mid = (v - hi).astype(BF16).astype(F32)
    low = (v - hi - mid).astype(BF16).astype(F32)
    return hi, mid, low


def pair(cols, at, lane):
    return jnp.where(lane < WIDTH, cols[:, at : at + 1], cols[:, at + 1 : at + 2])


def pair_decay(run, cols, h):
    diff = run[h : h + 1, :] - cols[:, h : h + 1]
    causal = iota((TOKENS, TOKENS), 1) >= iota((TOKENS, TOKENS), 0)
    return jnp.exp(jnp.where(causal, diff, -jnp.inf))


def expanded(ext):
    source, target = iota((128, COLS), 0), iota((128, COLS), 1)
    spread = (source < 3 * HEADS) & (source % HEADS == target // WIDTH)
    return dot(ext, jnp.where(spread, 1.0, 0.0).astype(BF16), 1, 0)


def weights_body(
    where_ref, x_hbm, dy_hbm, dt_hbm, ld_hbm, b_hbm, c_hbm, w_hbm,
    wx_ref, wdy_ref, run_ref, cols_hbm, ext_ref, b_ref, c_ref, w1_hbm, w3_hbm, w2_hbm, wx_hbm, wdy_hbm, fwd_hbm,
    x_ref, dy_ref, dt_ref, ld_ref, cols_ref, w_ref, fwd_ref, sems,
):
    rows, share = w1_hbm.shape
    down = pl.ds(pl.multiple_of(where_ref[0] * rows, rows), rows)
    pieces = [(ld_hbm, ld_ref), (dt_hbm, dt_ref), (x_hbm, x_ref), (dy_hbm, dy_ref), (b_hbm, b_ref), (c_hbm, c_ref)]
    for i, ahead in enumerate((1, 3, 2)):
        across = pl.ds(pl.multiple_of(lax.rem(where_ref[1] + ahead, 4) * share, share), share)
        pieces.append((w_hbm.at[down, across], w_ref.at[i]))
    late = fetch(pieces, sems)
    out = []

    def put(source, target):
        out.append(pltpu.make_async_copy(source, target, sems.at[len(pieces) + len(out)]))
        out[-1].start()

    late[0].wait()
    tri = jnp.where(iota((TOKENS, TOKENS), 0) <= iota((TOKENS, TOKENS), 1), 1.0, 0.0).astype(BF16)
    parts = jnp.concatenate(split3(ld_ref[...]), axis=0).astype(BF16)
    sums = dot(parts, tri, 1, 0)
    run = sums[:HEADS] + sums[HEADS : 2 * HEADS] + sums[2 * HEADS :]
    run_ref[...] = run
    late[1].wait()
    dt = dt_ref[...]
    end = run[:, TOKENS - 1 :]
    fwd = dt * jnp.exp(end - run)
    fwd_ref[...] = fwd
    put(fwd_ref, fwd_hbm)
    start = jnp.exp(run)
    stack = jnp.concatenate(
        [run, dt, fwd, start, jnp.zeros((128 - 4 * HEADS, TOKENS), F32)], axis=0
    )
    cols = stack.T
    cols_ref[...] = cols
    put(cols_ref, cols_hbm)

    hi, mid, low = split3(jnp.exp(end))
    lane8, row8 = iota((HEADS, 128), 1), iota((HEADS, 128), 0)
    spread = jnp.where(lane8 == row8, hi, 0.0)
    spread = spread + jnp.where(lane8 == row8 + HEADS, mid, 0.0)
    spread = spread + jnp.where(lane8 == row8 + 2 * HEADS, low, 0.0)
    ext_ref[...] = jnp.sum(spread, axis=0, keepdims=True)

    lane = iota((TOKENS, 128), 1)
    late[2].wait()
    for i in range(HEADS // 2):
        at = slice(128 * i, 128 * (i + 1))
        wx_ref[:, at] = (pair(cols, 2 * HEADS + 2 * i, lane) * x_ref[:, at].astype(F32)).astype(BF16)
    put(wx_ref, wx_hbm)
    late[3].wait()
    for i in range(HEADS // 2):
        at = slice(128 * i, 128 * (i + 1))
        wdy_ref[:, at] = (pair(cols, 3 * HEADS + 2 * i, lane) * dy_ref[:, at].astype(F32)).astype(BF16)
    put(wdy_ref, wdy_hbm)
    for copy in late[4:]:
        copy.wait()
    for k, w in enumerate((w1_hbm, w3_hbm, w2_hbm)):
        put(w_ref.at[k], w)
    for copy in out:
        copy.wait()


def whole(own_ref, other):
    return jnp.concatenate([own_ref[...], other], axis=0)


def pieces_out(source, target, at, sems, first):
    rows = source.shape[0] // 4
    parts = [slice(k * rows, (k + 1) * rows) for k in range(4)]
    return [pltpu.make_async_copy(source.at[r, at], target.at[r, at], sems.at[first + k]) for k, r in enumerate(parts)]


def ends_body(b_ref, c_ref, other_b, other_c, wx_ref, wdy_ref, ext_ref, send_hbm, send_ref, sems):
    early = pieces_out(send_ref, send_hbm, slice(0, COLS), sems, 0)
    late = pieces_out(send_ref, send_hbm, slice(COLS, 2 * COLS + 128), sems, 4)
    send_ref[:, :COLS] = dot(whole(b_ref, other_b[...]), wx_ref[...], 1, 0).astype(BF16)
    for copy in early:
        copy.start()
    send_ref[:, COLS : 2 * COLS] = dot(whole(c_ref, other_c[...]), wdy_ref[...], 1, 0).astype(BF16)
    send_ref[:, 2 * COLS :] = jnp.broadcast_to(ext_ref[...], (STATE, 128)).astype(BF16)
    for copy in late:
        copy.start()
    for copy in early + late:
        copy.wait()


def scan_body(got_ref, out_hbm, out_ref, decay_ref, sems):
    early = pieces_out(out_ref, out_hbm, slice(0, COLS), sems, 0)
    late = pieces_out(out_ref, out_hbm, slice(COLS, 2 * COLS), sems, 4)
    decay_ref[...] = expanded(got_ref[:, 2 * COLS :])
    two = 2 * LINES

    def place(chip):
        row = chip % 2 * (BLOCKS // 4) + chip // 2
        return slice(row * two, (row + 1) * two)

    state = jnp.zeros((LINES, COLS), F32)
    for c in range(BLOCKS // 2):
        at = place(c)
        term, decay = got_ref[at, :COLS].astype(F32), decay_ref[at, :]
        after = state * decay[:LINES] + term[:LINES]
        out_ref[at, :COLS] = jnp.concatenate([state, after], axis=0).astype(BF16)
        state = after * decay[LINES:] + term[LINES:]
    for copy in early:
        copy.start()
    state = jnp.zeros((LINES, COLS), F32)
    for c in range(BLOCKS // 2 - 1, -1, -1):
        at = place(c)
        term, decay = got_ref[at, COLS : 2 * COLS].astype(F32), decay_ref[at, :]
        before = state * decay[LINES:] + term[LINES:]
        out_ref[at, COLS:] = jnp.concatenate([before, state], axis=0).astype(BF16)
        state = before * decay[:LINES] + term[:LINES]
    for copy in late:
        copy.start()
    for copy in early + late:
        copy.wait()


def local_x_body(x_ref, dy_ref, b_ref, c_ref, other_b, other_c, run_ref, cols_ref, loc_ref, bt_ref, ms_ref):
    run, cols = run_ref[...], cols_ref[...]
    bt = whole(b_ref, other_b[...]).T
    bt_ref[...] = bt
    score = dot(bt, whole(c_ref, other_c[...]), 1, 0)
    lane = iota((TOKENS, 128), 1)
    total = jnp.zeros((TOKENS, TOKENS), F32)
    for i in range(HEADS // 2):
        at = slice(128 * i, 128 * (i + 1))
        xp, dyp = x_ref[:, at], dy_ref[:, at]
        local = []
        for k in range(2):
            h = 2 * i + k
            own = (lane < WIDTH) if k == 0 else (lane >= WIDTH)
            decay = pair_decay(run, cols, h)
            inter = dot(jnp.where(own, xp, jnp.zeros_like(xp)), dyp, 1, 1)
            mixing = (decay * inter * cols[:, HEADS + h : HEADS + h + 1]).astype(BF16)
            total = total + mixing.astype(F32)
            local.append(dot((decay * score).astype(BF16), dyp, 1, 0))
        local = pair(cols, HEADS + 2 * i, lane) * jnp.where(lane < WIDTH, local[0], local[1])
        loc_ref[:, at] = local.astype(BF16)
    ms_ref[...] = total.astype(BF16)


def grad_x_body(bt_hbm, fwd_hbm, loc_hbm, states_ref, gx_ref, bt_ref, fwd_ref, loc_ref, sems):
    early = fetch([(bt_hbm, bt_ref), (fwd_hbm, fwd_ref), (loc_hbm, loc_ref)], sems)
    lane = iota((TOKENS, 128), 1)
    early[1].wait()
    cols = jnp.concatenate([fwd_ref[...], jnp.zeros((128 - HEADS, TOKENS), F32)], axis=0).T
    early[0].wait()
    early[2].wait()
    for i in range(HEADS // 2):
        at = slice(128 * i, 128 * (i + 1))
        carried = dot(bt_ref[...], states_ref[:, COLS + 128 * i : COLS + 128 * (i + 1)], 1, 0)
        gx_ref[:, at] = (loc_ref[:, at].astype(F32) + pair(cols, 2 * i, lane) * carried).astype(BF16)


def grad_bc_body(b_ref, c_ref, other_b, other_c, ms_ref, wx_ref, wdy_ref, states_ref, keep_ref, send_ref):
    b_full, c_full = whole(b_ref, other_b[...]), whole(c_ref, other_c[...])
    part_b = (dot(c_full, ms_ref[...], 1, 1) + dot(states_ref[:, COLS:], wx_ref[...], 1, 1)).astype(BF16)
    part_c = (dot(b_full, ms_ref[...], 1, 0) + dot(states_ref[:, :COLS], wdy_ref[...], 1, 1)).astype(BF16)
    keep_ref[:HALF, :] = part_b[:HALF]
    keep_ref[HALF:, :] = part_c[:HALF]
    send_ref[:HALF, :] = part_b[HALF:]
    send_ref[HALF:, :] = part_c[HALF:]


def add_bc_body(mine_ref, got_ref, gb_ref, gc_ref):
    half = STATE // 2
    total = (mine_ref[...].astype(F32) + got_ref[...].astype(F32)).astype(BF16)
    gb_ref[...] = total[:half]
    gc_ref[...] = total[half:]


def pass_body(*refs):
    pass


def passed(*arrays):
    anywhere = [SPACES["a"]] * len(arrays)
    return pl.pallas_call(
        pass_body,
        out_shape=[jax.ShapeDtypeStruct(v.shape, v.dtype) for v in arrays],
        in_specs=anywhere,
        out_specs=anywhere,
        input_output_aliases={i: i for i in range(len(arrays))},
        compiler_params=pltpu.CompilerParams(vmem_limit_bytes=LIMIT),
        cost_estimate=pl.CostEstimate(flops=PASS_FLOPS, bytes_accessed=2**20, transcendentals=0),
    )(*arrays)


def load_body(where_ref, w_hbm, *refs):
    *pieces, w_ref, sems = refs
    core, here, share, half = where_ref[0], where_ref[1], w_ref.shape[1], COLS // 2
    pairs = [(w_hbm.at[:, pl.ds(pl.multiple_of(here * share, share), share)], w_ref.at[:COLS, :])]
    for i, piece in enumerate(pieces):
        side = core if i < 3 else 1 - core
        start = pl.multiple_of((i % 3 + 1) * COLS + side * half, half)
        pairs.append((piece, w_ref.at[pl.ds(start, half), :]))
    for copy in fetch(pairs, sems):
        copy.wait()


def project_body(w_ref, *refs):
    *gx_refs, out_hbm, tiles_ref, sems = refs
    tile = out_hbm.shape[2]
    late = []
    for j in range(out_hbm.shape[0]):
        total = jnp.zeros((TOKENS, tile), F32)
        for k, gx_ref in enumerate(gx_refs):
            total = total + dot(gx_ref[...], w_ref[k * COLS : (k + 1) * COLS, j * tile : (j + 1) * tile], 1, 0)
        tiles_ref[j] = total.astype(BF16)
        copy = pltpu.make_async_copy(tiles_ref.at[j], out_hbm.at[j], sems.at[j])
        copy.start()
        late.append(copy)
    for copy in late:
        copy.wait()


def add_y_body(got_ref, out_ref):
    total = got_ref[0].astype(F32)
    for k in range(1, got_ref.shape[0]):
        total = total + got_ref[k].astype(F32)
    out_ref[...] = total.T.astype(BF16)


def per_device(x_in, grad_out, step_size, log_decay, b_proj, c_proj, w_in):
    hold = lax.optimization_barrier
    core, x_index = lax.axis_index("core"), lax.axis_index("x")
    flip = [(i, i ^ 1) for i in range(lax.axis_size("yh"))]
    half = w_in.shape[0] // 2
    share = w_in.shape[1] // 4
    square, wide, own_half = (TOKENS, TOKENS), (TOKENS, COLS), (HALF, TOKENS)

    def ahead_on_x(shard, ahead):
        return lax.ppermute(shard, "x", [(i, (i + ahead) % 4) for i in range(4)])

    def other_core(shard):
        return lax.ppermute(shard, "core", [(0, 1), (1, 0)])

    where = jnp.stack([core, x_index])
    bc = lax.ppermute(b_proj, "yh", flip), lax.ppermute(c_proj, "yh", flip)
    wx, wdy, run, cols, ext, b_own, c_own, w_next, w_prev, w_far, wx_late, wdy_late, fwd = call(
        weights_body,
        "shhhhhhh",
        [(wide, BF16), (wide, BF16), ((HEADS, TOKENS), F32), ((TOKENS, 128), F32), ((1, 128), F32)]
        + [(own_half, BF16)] * 2
        + [((half, share), BF16)] * 3
        + [(wide, BF16)] * 2
        + [((HEADS, TOKENS), F32)],
        [(wide, BF16), (wide, BF16), ((HEADS, TOKENS), F32), ((HEADS, TOKENS), F32)]
        + [((TOKENS, 128), F32), ((3, half, share), BF16), ((HEADS, TOKENS), F32)],
        copies=16,
        out_spaces="vvvhvvvhhhhhh",
    )(where, x_in, grad_out, step_size, log_decay, b_proj, c_proj, w_in)
    ends = ((STATE, 2 * COLS + 128), BF16)
    (send,) = call(ends_body, "vvvvvvv", [ends], [ends], copies=8, out_spaces="h")(b_own, c_own, *bc, wx, wdy, ext)

    terms = lax.all_to_all(send, EXCHANGE, 0, 0, tiled=True)
    w_next, w_prev, w_far, bc, _ = hold((w_next, w_prev, w_far, bc, send))
    w_prev, w_next, w_far = ahead_on_x(w_next, 1), ahead_on_x(w_prev, 3), ahead_on_x(w_far, 2)
    local_x, b_rows, mixed = call(
        local_x_body, "bbbbvvvb", [(wide, BF16), (square, BF16), (square, BF16)], out_spaces="bbb"
    )(x_in, grad_out, b_proj, c_proj, *bc, run, cols)
    terms, local_x, b_rows, mixed = hold((terms, local_x, b_rows, mixed))
    both = ((STATE, 2 * COLS), BF16)
    (scanned,) = call(scan_body, "v", [both], [both, ((STATE, COLS), F32)], copies=8, out_spaces="h")(terms)
    states = lax.all_to_all(scanned, EXCHANGE, 0, 0, tiled=True)
    w_prev, w_far, w_next, _ = hold((w_prev, w_far, w_next, scanned))
    w_mine = passed(w_prev, w_far, w_next)
    w_theirs = [other_core(w) for w in w_mine]
    states, w_mine, w_theirs = hold((states, w_mine, w_theirs))

    (gx,) = call(
        grad_x_body, "hhhv", [(wide, BF16)], [(square, BF16), ((HEADS, TOKENS), F32), (wide, BF16)], copies=3, out_spaces="v"
    )(b_rows, fwd, local_x, states)
    gx_far = ahead_on_x(gx, 2)
    gx_prev, gx_next = ahead_on_x(gx, 1), ahead_on_x(gx, 3)
    states, w_mine, _ = hold((states, w_mine, gx))
    keep_bc, send_bc = call(grad_bc_body, "bbvvbbbv", [(square, BF16), (square, BF16)], out_spaces="vv")(
        b_proj, c_proj, *bc, mixed, wx_late, wdy_late, states
    )
    got_bc = lax.ppermute(send_bc, "yh", flip)
    (w_here,) = call(load_body, "shhhhhhh", [((4 * COLS, share), BF16)], copies=7, out_spaces="V")(
        where, w_in, *w_mine, *w_theirs
    )
    gx_prev, gx_far, gx_next, w_here = hold((gx_prev, gx_far, gx_next, w_here))

    four = ((4, *square), BF16)
    (partial,) = call(project_body, "Vvvvv", [four], [four], copies=4, out_spaces="h")(
        w_here, gx, gx_prev, gx_far, gx_next
    )
    over_y = lax.all_to_all(partial, "yh", 0, 0, tiled=True)
    (grad_input,) = call(add_y_body, "v", [(square, BF16)], out_spaces="v")(over_y)
    grad_b, grad_c = call(
        add_bc_body, "vv", [(own_half, BF16), (own_half, BF16)], out_spaces="vv", flops=ADD_FLOPS
    )(keep_bc, got_bc)
    return grad_input, grad_b, grad_c


def solution(mesh):
    fine = Mesh(mesh.devices.reshape(8, 2, 2, 4, 4), CONTEXT + TENSOR)
    by_token, by_head = P(CONTEXT, TENSOR), P(TENSOR, CONTEXT)
    return jax.shard_map(
        per_device,
        mesh=fine,
        in_specs=(by_token, by_token, by_head, by_head, by_head, by_head, P(TENSOR, None)),
        out_specs=(by_head, by_head, by_head),
        check_vma=False,
    )
```

```python
import jax
import jax.numpy as jnp
from jax import lax
from jax.experimental import pallas as pl
from jax.experimental.pallas import tpu as pltpu
from jax.sharding import Mesh, PartitionSpec as P

CONTEXT = ("z", "yl", "core")
EXCHANGE = ("yl", "z", "core")
TENSOR = ("x", "yh")
F32 = jnp.float32
BF16 = jnp.bfloat16
HEADS = 8
WIDTH = 64
TOKENS = 256
STATE = 256
COLS = HEADS * WIDTH
HALF = STATE // 2
BLOCKS = 32
LINES = STATE // BLOCKS


SPACES = {
    "s": pl.BlockSpec(memory_space=pltpu.SMEM),
    "v": pl.BlockSpec(memory_space=pltpu.VMEM),
    "V": pl.BlockSpec(memory_space=pltpu.VMEM),
    "b": pl.BlockSpec(memory_space=pltpu.VMEM),
    "h": pl.BlockSpec(memory_space=pltpu.HBM),
    "a": pl.BlockSpec(memory_space=pl.ANY),
}
PLACES = {"h": pltpu.HBM, "b": pltpu.HBM, "V": pltpu.VMEM}
ADD_FLOPS = 10 * 10**9
PASS_FLOPS = 4 * 10**9
LIMIT = 16 * 1024 * 1024


def call(body, spaces, outs, scratch=(), copies=0, out_spaces="", flops=10**9):
    run = pl.pallas_call(
        body,
        out_shape=[
            PLACES[k](s, d) if k in PLACES else jax.ShapeDtypeStruct(s, d)
            for (s, d), k in zip(outs, out_spaces or "V" * len(outs))
        ],
        in_specs=[SPACES[k] for k in spaces],
        out_specs=[SPACES[k] for k in out_spaces or "V" * len(outs)],
        scratch_shapes=[pltpu.VMEM(s, d) for s, d in scratch]
        + ([pltpu.SemaphoreType.DMA((copies,))] if copies else []),
        compiler_params=pltpu.CompilerParams(vmem_limit_bytes=LIMIT),
        cost_estimate=pl.CostEstimate(flops=flops, bytes_accessed=2**20, transcendentals=0),
    )

    def pinned(*args):
        return run(
            *(pltpu.with_memory_space_constraint(a, PLACES[k]) if k in PLACES else a for a, k in zip(args, spaces))
        )

    return pinned


def fetch(pairs, sems):
    copies = [pltpu.make_async_copy(a, b, sems.at[i]) for i, (a, b) in enumerate(pairs)]
    for copy in copies:
        copy.start()
    return copies


def iota(shape, dim):
    return lax.broadcasted_iota(jnp.int32, shape, dim)


def dot(a, b, ca, cb):
    return lax.dot_general(a, b, (((ca,), (cb,)), ((), ())), preferred_element_type=F32)


def split3(v):
    hi = v.astype(BF16).astype(F32)
    mid = (v - hi).astype(BF16).astype(F32)
    low = (v - hi - mid).astype(BF16).astype(F32)
    return hi, mid, low


def pair(cols, at, lane):
    return jnp.where(lane < WIDTH, cols[:, at : at + 1], cols[:, at + 1 : at + 2])


def pair_decay(run, cols, h):
    diff = run[h : h + 1, :] - cols[:, h : h + 1]
    causal = iota((TOKENS, TOKENS), 1) >= iota((TOKENS, TOKENS), 0)
    return jnp.exp(jnp.where(causal, diff, -jnp.inf))


def expanded(ext):
    source, target = iota((128, COLS), 0), iota((128, COLS), 1)
    spread = (source < 3 * HEADS) & (source % HEADS == target // WIDTH)
    return dot(ext, jnp.where(spread, 1.0, 0.0).astype(BF16), 1, 0)


def weights_body(
    where_ref, x_hbm, dy_hbm, dt_hbm, ld_hbm, b_hbm, c_hbm, w_hbm,
    wx_ref, wdy_ref, run_ref, cols_hbm, ext_ref, b_ref, c_ref, w1_hbm, w3_hbm, w2_hbm, wx_hbm, wdy_hbm, fwd_hbm,
    x_ref, dy_ref, dt_ref, ld_ref, cols_ref, w_ref, fwd_ref, sems,
):
    rows, share = w1_hbm.shape
    down = pl.ds(pl.multiple_of(where_ref[0] * rows, rows), rows)
    pieces = [(ld_hbm, ld_ref), (dt_hbm, dt_ref), (x_hbm, x_ref), (dy_hbm, dy_ref), (b_hbm, b_ref), (c_hbm, c_ref)]
    for i, ahead in enumerate((1, 3, 2)):
        across = pl.ds(pl.multiple_of(lax.rem(where_ref[1] + ahead, 4) * share, share), share)
        pieces.append((w_hbm.at[down, across], w_ref.at[i]))
    late = fetch(pieces, sems)
    out = []

    def put(source, target):
        out.append(pltpu.make_async_copy(source, target, sems.at[len(pieces) + len(out)]))
        out[-1].start()

    late[0].wait()
    tri = jnp.where(iota((TOKENS, TOKENS), 0) <= iota((TOKENS, TOKENS), 1), 1.0, 0.0).astype(BF16)
    parts = jnp.concatenate(split3(ld_ref[...]), axis=0).astype(BF16)
    sums = dot(parts, tri, 1, 0)
    run = sums[:HEADS] + sums[HEADS : 2 * HEADS] + sums[2 * HEADS :]
    run_ref[...] = run
    late[1].wait()
    dt = dt_ref[...]
    end = run[:, TOKENS - 1 :]
    fwd = dt * jnp.exp(end - run)
    fwd_ref[...] = fwd
    put(fwd_ref, fwd_hbm)
    start = jnp.exp(run)
    stack = jnp.concatenate(
        [run, dt, fwd, start, jnp.zeros((128 - 4 * HEADS, TOKENS), F32)], axis=0
    )
    cols = stack.T
    cols_ref[...] = cols
    put(cols_ref, cols_hbm)

    hi, mid, low = split3(jnp.exp(end))
    lane8, row8 = iota((HEADS, 128), 1), iota((HEADS, 128), 0)
    spread = jnp.where(lane8 == row8, hi, 0.0)
    spread = spread + jnp.where(lane8 == row8 + HEADS, mid, 0.0)
    spread = spread + jnp.where(lane8 == row8 + 2 * HEADS, low, 0.0)
    ext_ref[...] = jnp.sum(spread, axis=0, keepdims=True)

    lane = iota((TOKENS, 128), 1)
    late[2].wait()
    for i in range(HEADS // 2):
        at = slice(128 * i, 128 * (i + 1))
        wx_ref[:, at] = (pair(cols, 2 * HEADS + 2 * i, lane) * x_ref[:, at].astype(F32)).astype(BF16)
    put(wx_ref, wx_hbm)
    late[3].wait()
    for i in range(HEADS // 2):
        at = slice(128 * i, 128 * (i + 1))
        wdy_ref[:, at] = (pair(cols, 3 * HEADS + 2 * i, lane) * dy_ref[:, at].astype(F32)).astype(BF16)
    put(wdy_ref, wdy_hbm)
    for copy in late[4:]:
        copy.wait()
    for k, w in enumerate((w1_hbm, w3_hbm, w2_hbm)):
        put(w_ref.at[k], w)
    for copy in out:
        copy.wait()


def whole(own_ref, other):
    return jnp.concatenate([own_ref[...], other], axis=0)


def ends_body(b_ref, c_ref, other_b, other_c, wx_ref, wdy_ref, ext_ref, send_hbm, send_ref, sems):
    parts = [slice(0, COLS), slice(COLS, 2 * COLS + 128)]
    copies = [pltpu.make_async_copy(send_ref.at[:, at], send_hbm.at[:, at], sems.at[i]) for i, at in enumerate(parts)]
    send_ref[:, :COLS] = dot(whole(b_ref, other_b[...]), wx_ref[...], 1, 0).astype(BF16)
    copies[0].start()
    send_ref[:, COLS : 2 * COLS] = dot(whole(c_ref, other_c[...]), wdy_ref[...], 1, 0).astype(BF16)
    send_ref[:, 2 * COLS :] = jnp.broadcast_to(ext_ref[...], (STATE, 128)).astype(BF16)
    copies[1].start()
    for copy in copies:
        copy.wait()


def scan_body(got_ref, out_hbm, out_ref, decay_ref, sems):
    halves = [slice(0, COLS), slice(COLS, 2 * COLS)]
    copies = [pltpu.make_async_copy(out_ref.at[:, at], out_hbm.at[:, at], sems.at[i]) for i, at in enumerate(halves)]
    decay_ref[...] = expanded(got_ref[:, 2 * COLS :])
    two = 2 * LINES

    def place(chip):
        row = chip % 2 * (BLOCKS // 4) + chip // 2
        return slice(row * two, (row + 1) * two)

    state = jnp.zeros((LINES, COLS), F32)
    for c in range(BLOCKS // 2):
        at = place(c)
        term, decay = got_ref[at, :COLS].astype(F32), decay_ref[at, :]
        after = state * decay[:LINES] + term[:LINES]
        out_ref[at, :COLS] = jnp.concatenate([state, after], axis=0).astype(BF16)
        state = after * decay[LINES:] + term[LINES:]
    copies[0].start()
    state = jnp.zeros((LINES, COLS), F32)
    for c in range(BLOCKS // 2 - 1, -1, -1):
        at = place(c)
        term, decay = got_ref[at, COLS : 2 * COLS].astype(F32), decay_ref[at, :]
        before = state * decay[LINES:] + term[LINES:]
        out_ref[at, COLS:] = jnp.concatenate([before, state], axis=0).astype(BF16)
        state = before * decay[:LINES] + term[:LINES]
    copies[1].start()
    for copy in copies:
        copy.wait()


def local_x_body(x_ref, dy_ref, b_ref, c_ref, other_b, other_c, run_ref, cols_ref, loc_ref, bt_ref, ms_ref):
    run, cols = run_ref[...], cols_ref[...]
    bt = whole(b_ref, other_b[...]).T
    bt_ref[...] = bt
    score = dot(bt, whole(c_ref, other_c[...]), 1, 0)
    lane = iota((TOKENS, 128), 1)
    total = jnp.zeros((TOKENS, TOKENS), F32)
    for i in range(HEADS // 2):
        at = slice(128 * i, 128 * (i + 1))
        xp, dyp = x_ref[:, at], dy_ref[:, at]
        local = []
        for k in range(2):
            h = 2 * i + k
            own = (lane < WIDTH) if k == 0 else (lane >= WIDTH)
            decay = pair_decay(run, cols, h)
            inter = dot(jnp.where(own, xp, jnp.zeros_like(xp)), dyp, 1, 1)
            mixing = (decay * inter * cols[:, HEADS + h : HEADS + h + 1]).astype(BF16)
            total = total + mixing.astype(F32)
            local.append(dot((decay * score).astype(BF16), dyp, 1, 0))
        local = pair(cols, HEADS + 2 * i, lane) * jnp.where(lane < WIDTH, local[0], local[1])
        loc_ref[:, at] = local.astype(BF16)
    ms_ref[...] = total.astype(BF16)


def grad_x_body(bt_hbm, fwd_hbm, loc_hbm, states_ref, gx_ref, bt_ref, fwd_ref, loc_ref, sems):
    early = fetch([(bt_hbm, bt_ref), (fwd_hbm, fwd_ref), (loc_hbm, loc_ref)], sems)
    lane = iota((TOKENS, 128), 1)
    early[1].wait()
    cols = jnp.concatenate([fwd_ref[...], jnp.zeros((128 - HEADS, TOKENS), F32)], axis=0).T
    early[0].wait()
    early[2].wait()
    for i in range(HEADS // 2):
        at = slice(128 * i, 128 * (i + 1))
        carried = dot(bt_ref[...], states_ref[:, COLS + 128 * i : COLS + 128 * (i + 1)], 1, 0)
        gx_ref[:, at] = (loc_ref[:, at].astype(F32) + pair(cols, 2 * i, lane) * carried).astype(BF16)


def grad_bc_body(b_ref, c_ref, other_b, other_c, ms_ref, wx_ref, wdy_ref, states_ref, keep_ref, send_ref):
    b_full, c_full = whole(b_ref, other_b[...]), whole(c_ref, other_c[...])
    part_b = (dot(c_full, ms_ref[...], 1, 1) + dot(states_ref[:, COLS:], wx_ref[...], 1, 1)).astype(BF16)
    part_c = (dot(b_full, ms_ref[...], 1, 0) + dot(states_ref[:, :COLS], wdy_ref[...], 1, 1)).astype(BF16)
    keep_ref[:HALF, :] = part_b[:HALF]
    keep_ref[HALF:, :] = part_c[:HALF]
    send_ref[:HALF, :] = part_b[HALF:]
    send_ref[HALF:, :] = part_c[HALF:]


def add_bc_body(mine_ref, got_ref, gb_ref, gc_ref):
    half = STATE // 2
    total = (mine_ref[...].astype(F32) + got_ref[...].astype(F32)).astype(BF16)
    gb_ref[...] = total[:half]
    gc_ref[...] = total[half:]


def pass_body(*refs):
    pass


def passed(*arrays):
    anywhere = [SPACES["a"]] * len(arrays)
    return pl.pallas_call(
        pass_body,
        out_shape=[jax.ShapeDtypeStruct(v.shape, v.dtype) for v in arrays],
        in_specs=anywhere,
        out_specs=anywhere,
        input_output_aliases={i: i for i in range(len(arrays))},
        compiler_params=pltpu.CompilerParams(vmem_limit_bytes=LIMIT),
        cost_estimate=pl.CostEstimate(flops=PASS_FLOPS, bytes_accessed=2**20, transcendentals=0),
    )(*arrays)


def load_body(where_ref, w_hbm, *refs):
    *pieces, w_ref, sems = refs
    core, here, share, half = where_ref[0], where_ref[1], w_ref.shape[1], COLS // 2
    pairs = [(w_hbm.at[:, pl.ds(pl.multiple_of(here * share, share), share)], w_ref.at[:COLS, :])]
    for i, piece in enumerate(pieces):
        side = core if i < 3 else 1 - core
        start = pl.multiple_of((i % 3 + 1) * COLS + side * half, half)
        pairs.append((piece, w_ref.at[pl.ds(start, half), :]))
    for copy in fetch(pairs, sems):
        copy.wait()


def project_body(w_ref, *refs):
    *gx_refs, out_hbm, tiles_ref, sems = refs
    tile = out_hbm.shape[2]
    late = []
    for j in range(out_hbm.shape[0]):
        total = jnp.zeros((TOKENS, tile), F32)
        for k, gx_ref in enumerate(gx_refs):
            total = total + dot(gx_ref[...], w_ref[k * COLS : (k + 1) * COLS, j * tile : (j + 1) * tile], 1, 0)
        tiles_ref[j] = total.astype(BF16)
        copy = pltpu.make_async_copy(tiles_ref.at[j], out_hbm.at[j], sems.at[j])
        copy.start()
        late.append(copy)
    for copy in late:
        copy.wait()


def add_y_body(got_ref, out_ref):
    total = got_ref[0].astype(F32)
    for k in range(1, got_ref.shape[0]):
        total = total + got_ref[k].astype(F32)
    out_ref[...] = total.T.astype(BF16)


def per_device(x_in, grad_out, step_size, log_decay, b_proj, c_proj, w_in):
    hold = lax.optimization_barrier
    core, x_index = lax.axis_index("core"), lax.axis_index("x")
    flip = [(i, i ^ 1) for i in range(lax.axis_size("yh"))]
    half = w_in.shape[0] // 2
    share = w_in.shape[1] // 4
    square, wide, own_half = (TOKENS, TOKENS), (TOKENS, COLS), (HALF, TOKENS)

    def ahead_on_x(shard, ahead):
        return lax.ppermute(shard, "x", [(i, (i + ahead) % 4) for i in range(4)])

    def other_core(shard):
        return lax.ppermute(shard, "core", [(0, 1), (1, 0)])

    where = jnp.stack([core, x_index])
    bc = lax.ppermute(b_proj, "yh", flip), lax.ppermute(c_proj, "yh", flip)
    wx, wdy, run, cols, ext, b_own, c_own, w_next, w_prev, w_far, wx_late, wdy_late, fwd = call(
        weights_body,
        "shhhhhhh",
        [(wide, BF16), (wide, BF16), ((HEADS, TOKENS), F32), ((TOKENS, 128), F32), ((1, 128), F32)]
        + [(own_half, BF16)] * 2
        + [((half, share), BF16)] * 3
        + [(wide, BF16)] * 2
        + [((HEADS, TOKENS), F32)],
        [(wide, BF16), (wide, BF16), ((HEADS, TOKENS), F32), ((HEADS, TOKENS), F32)]
        + [((TOKENS, 128), F32), ((3, half, share), BF16), ((HEADS, TOKENS), F32)],
        copies=16,
        out_spaces="vvvhvvvhhhhhh",
    )(where, x_in, grad_out, step_size, log_decay, b_proj, c_proj, w_in)
    ends = ((STATE, 2 * COLS + 128), BF16)
    (send,) = call(ends_body, "vvvvvvv", [ends], [ends], copies=2, out_spaces="h")(b_own, c_own, *bc, wx, wdy, ext)

    terms = lax.all_to_all(send, EXCHANGE, 0, 0, tiled=True)
    w_next, w_prev, w_far, bc, _ = hold((w_next, w_prev, w_far, bc, send))
    w_prev, w_next, w_far = ahead_on_x(w_next, 1), ahead_on_x(w_prev, 3), ahead_on_x(w_far, 2)
    local_x, b_rows, mixed = call(
        local_x_body, "bbbbvvvb", [(wide, BF16), (square, BF16), (square, BF16)], out_spaces="bbb"
    )(x_in, grad_out, b_proj, c_proj, *bc, run, cols)
    terms, local_x, b_rows, mixed = hold((terms, local_x, b_rows, mixed))
    both = ((STATE, 2 * COLS), BF16)
    (scanned,) = call(scan_body, "v", [both], [both, ((STATE, COLS), F32)], copies=2, out_spaces="h")(terms)
    states = lax.all_to_all(scanned, EXCHANGE, 0, 0, tiled=True)
    w_prev, w_far, w_next, _ = hold((w_prev, w_far, w_next, scanned))
    w_prev, w_next, w_far = passed(w_prev, w_next, w_far)
    w_mine = [w_prev, w_far, w_next]
    w_theirs = [other_core(w) for w in w_mine]
    states, w_mine, w_theirs = hold((states, w_mine, w_theirs))

    (gx,) = call(
        grad_x_body, "hhhv", [(wide, BF16)], [(square, BF16), ((HEADS, TOKENS), F32), (wide, BF16)], copies=3, out_spaces="v"
    )(b_rows, fwd, local_x, states)
    gx_far = ahead_on_x(gx, 2)
    gx_prev, gx_next = ahead_on_x(gx, 1), ahead_on_x(gx, 3)
    states, w_mine, _ = hold((states, w_mine, gx))
    keep_bc, send_bc = call(grad_bc_body, "bbvvbbbv", [(square, BF16), (square, BF16)], out_spaces="vv")(
        b_proj, c_proj, *bc, mixed, wx_late, wdy_late, states
    )
    got_bc = lax.ppermute(send_bc, "yh", flip)
    (w_here,) = call(load_body, "shhhhhhh", [((4 * COLS, share), BF16)], copies=7, out_spaces="V")(
        where, w_in, *w_mine, *w_theirs
    )
    gx_prev, gx_far, gx_next, w_here = hold((gx_prev, gx_far, gx_next, w_here))

    four = ((4, *square), BF16)
    (partial,) = call(project_body, "Vvvvv", [four], [four], copies=4, out_spaces="h")(
        w_here, gx, gx_prev, gx_far, gx_next
    )
    over_y = lax.all_to_all(partial, "yh", 0, 0, tiled=True)
    (grad_input,) = call(add_y_body, "v", [(square, BF16)], out_spaces="v")(over_y)
    grad_b, grad_c = call(
        add_bc_body, "vv", [(own_half, BF16), (own_half, BF16)], out_spaces="vv", flops=ADD_FLOPS
    )(keep_bc, got_bc)
    return grad_input, grad_b, grad_c


def solution(mesh):
    fine = Mesh(mesh.devices.reshape(8, 2, 2, 4, 4), CONTEXT + TENSOR)
    by_token, by_head = P(CONTEXT, TENSOR), P(TENSOR, CONTEXT)
    return jax.shard_map(
        per_device,
        mesh=fine,
        in_specs=(by_token, by_token, by_head, by_head, by_head, by_head, P(TENSOR, None)),
        out_specs=(by_head, by_head, by_head),
        check_vma=False,
    )
```
